256 devices in a mesh: dp: 64 (over x, z, core), mp: 4 (over y).
Axes of the slice: x: 4, y: 4, z: 8, core: 2. Of those that a mesh axis runs over, the one named last changes fastest.
Arguments:
- grads: bfloat16 [64, 64, 512, 512], P('dp', None, None, 'mp'), may hold values from -6 to 6
- left_stats: float32 [64, 2, 512, 512], P('dp'), as said below
- right_stats: float32 [64, 2, 512, 512], P('dp'), as said below
- owners: int32 [64], replicated, may hold values from 0 to 63, as said below
- slots: int32 [64], replicated, may hold values from 0 to 1, as said below
Outputs:
- directions: bfloat16 [64, 512, 512], P(None, 'dp', 'mp')
The draws below stay inside these ranges and needn't reach their ends.
Inputs may be any that keep to these rules, and one draw needn't show every extreme that they name: `owners`: no two blocks share an owner and slot; some owner holds 2 blocks. `slots`: the slot of a block at its owner. `left_stats`: symmetric with a positive diagonal larger than the sum of magnitudes of its row's other entries. `right_stats`: symmetric with a positive diagonal larger than the sum of magnitudes of its row's other entries.
All inputs are finite; a program needn't handle non-finite values.
Results may differ from the reference program's by a relative error of at most 0.001.
Values may be sent and summed in bfloat16 or wider, within the bound.
A program may use at most 128 MiB of HBM per device.

```python
import jax
import jax.numpy as jnp
from jax import lax

B = 512
CAP = 2
POWER = 6
BLOCKS = 64
N_DP = 64


def bring_to(order_ids, value, place):
    position = jnp.argmax(order_ids == value).astype(jnp.int32)
    current = order_ids[place]
    return order_ids.at[position].set(current).at[place].set(value)


def placement_lists(key):
    orders = jax.random.permutation(jax.random.fold_in(key, 5), N_DP).astype(jnp.int32)
    orders = bring_to(orders, N_DP - 1, 0)
    orders = bring_to(orders, 0, 1)
    flips = jax.random.randint(jax.random.fold_in(key, 7), (N_DP,), 0, CAP)
    index = jnp.arange(BLOCKS, dtype=jnp.int32)
    owner_ids = orders[index // CAP].astype(jnp.int32)
    picked = flips[owner_ids]
    slot_ids = (index % CAP + picked) % CAP
    return (owner_ids, slot_ids.astype(jnp.int32))


def dominant_stats(key, lowest, highest):
    shape = (N_DP, CAP, B, B)
    spread = 0.02
    other = jax.random.uniform(jax.random.fold_in(key, 11), shape, jnp.float32, -spread, spread)
    other = 0.5 * (other + jnp.swapaxes(other, -1, -2))
    diag = jnp.exp(jax.random.uniform(jax.random.fold_in(key, 12), shape[:-1], jnp.float32, jnp.log(lowest), jnp.log(highest))) * B * spread
    eye = jnp.eye(B, dtype=jnp.float32)
    return other * (1.0 - eye) + diag[..., None] * eye


def draw_owners(key, part):
    owner_ids, slot_ids = placement_lists(key)
    return owner_ids


def draw_slots(key, part):
    owner_ids, slot_ids = placement_lists(key)
    return slot_ids


def draw_left_stats(key, part):
    key = jax.random.fold_in(key, 1)
    return dominant_stats(key, 0.6, 2.0)


def draw_right_stats(key, part):
    key = jax.random.fold_in(key, 2)
    return dominant_stats(key, 0.6, 2.0)


def block_levels(key, dims, cuts, low, top_value):
    loudness = 1.0
    for dim, shards_of in cuts:
        draws = jax.random.uniform(jax.random.fold_in(jax.random.fold_in(key, 6), dim), (shards_of,), jnp.float32, low / len(cuts), top_value / len(cuts))
        loudness = loudness * jnp.repeat(jnp.exp(draws), dims[dim] // shards_of).reshape((-1,) + (1,) * (len(dims) - 1 - dim))
    return loudness


def bell_draw(key, dims, scale, reach, split=(), kind=jnp.bfloat16):
    array = scale * jax.random.normal(key, dims, jnp.float32)
    if split:
        array = array * block_levels(key, dims, split, -0.22, 0.18)
    return jnp.clip(array, -reach, reach).astype(kind)


def setup_inputs(seed: int = 0) -> dict:
    splits = jax.random.split(jax.random.key(seed), 6)
    grads = bell_draw(splits[0], (N_DP, BLOCKS, B, B), 1.0, 6.0, ((0, 64), (3, 4)))
    left_stats = draw_left_stats(jax.random.fold_in(splits[5], 71), 0)
    right_stats = draw_right_stats(jax.random.fold_in(splits[5], 71), 0)
    owners = draw_owners(jax.random.fold_in(splits[5], 71), 0)
    slots = draw_slots(jax.random.fold_in(splits[5], 71), 0)
    return dict(grads=grads, left_stats=left_stats, right_stats=right_stats, owners=owners, slots=slots)


def matmul(a, b):
    return jnp.matmul(a, b, precision=lax.Precision.HIGHEST)

def matvec(stat, vector):
    return jnp.einsum('...ij,...j->...i', stat, vector, precision=lax.Precision.HIGHEST)

def inverse_root(stat):
    order = stat.shape[-1]
    eye = jnp.eye(order, dtype=jnp.float32)
    vector = jnp.full(stat.shape[:-1], order ** (-0.5), jnp.float32)
    for step in range(POWER):
        image = matvec(stat, vector)
        vector = image / jnp.sqrt(lax.optimization_barrier(jnp.sum(image * image, axis=-1, keepdims=True)))
    largest = lax.optimization_barrier(jnp.sum(vector * matvec(stat, vector), axis=-1))[..., None, None]
    factor = 2.5 / largest
    first = factor * stat
    tfirst = (5.0 * eye - first) / 4.0
    tsquare = matmul(tfirst, tfirst)
    tfourth = matmul(tsquare, tsquare)
    second = matmul(tfourth, first)
    xfirst = factor ** 0.25 * tfirst
    tsecond = (5.0 * eye - second) / 4.0
    return matmul(xfirst, tsecond)

def one_block(gmean, left_old, right_old):
    left_new = 0.95 * left_old + matmul(gmean, gmean.T)
    right_new = 0.95 * right_old + matmul(gmean.T, gmean)
    precond = matmul(matmul(inverse_root(left_new), gmean), inverse_root(right_new))
    ratio = jnp.sqrt((jnp.sum(gmean * gmean) + 1e-06) / (jnp.sum(precond * precond) + 1e-06))
    return (precond * ratio).astype(jnp.bfloat16)

def reference(grads, left_stats, right_stats, owners, slots):

    def accumulate(total, piece):
        return (total + piece.astype(jnp.float32), None)
    zeros = jnp.zeros(grads.shape[1:], jnp.float32)
    summed, unused = lax.scan(accumulate, zeros, grads)
    gmean = summed / N_DP

    def per_block(index):
        owner = owners[index]
        slot = slots[index]
        return one_block(gmean[index], left_stats[owner, slot], right_stats[owner, slot])
    return lax.map(per_block, jnp.arange(BLOCKS, dtype=jnp.int32))
```

```python
import jax
import jax.numpy as jnp
from jax import lax
from jax.experimental import pallas as pl
from jax.experimental.pallas import tpu as pltpu
from jax.sharding import PartitionSpec as P

CAP = 2
NX, NZ, NY = 4, 8, 4
MESH = pl.DeviceIdType.MESH
F32 = jnp.float32
BF16 = jnp.bfloat16


def place():
    dp = lax.axis_index("dp")
    chip = dp // 2
    return chip // NZ, chip % NZ, dp % 2, lax.axis_index("mp")


def device(x, z, c, y):
    return ((x * NZ + z) * 2 + c, y)


class Ring:
    def __init__(self, n, right, left, inbox, outbox, send, recv, local):
        self.n, self.to = n, (right, left)
        self.inbox, self.outbox, self.send, self.recv, self.local = inbox, outbox, send, recv, local
        self.count = n - 1

    def copy(self, way, m):
        return pltpu.make_async_remote_copy(
            src_ref=self.outbox.at[way, m],
            dst_ref=self.inbox.at[way, m],
            send_sem=self.send.at[way, m],
            recv_sem=self.recv.at[way, m],
            device_id=self.to[way],
            device_id_type=MESH,
        )

    def emit(self, m):
        hops = self.n // 2 - (m + 1) // 2
        for way in (0, 1):
            half = way if m % 2 == 0 else 1 - way
            step = hops if way == 0 else self.n - hops
            if m >= 2:
                self.copy(way, m - 2).wait_recv()

            def body(i, _):
                value = self.local(step, half * 16 + i)
                if m >= 2:
                    value = value + self.inbox[way, m - 2, i]
                self.outbox[way, m, i] = value
                return 0

            lax.fori_loop(0, 16, body, 0)
            self.copy(way, m).start()

    def finish(self, store):
        last = self.count - 1
        for way in (0, 1):
            for m in (last - 1, last):
                self.copy(way, m).wait_recv()
        for half in (0, 1):
            first = last if half == 0 else last - 1
            second = last - 1 if half == 0 else last

            def body(i, _):
                value = self.local(0, half * 16 + i)
                value = value + self.inbox[0, first, i] + self.inbox[1, second, i]
                store(half * 16 + i, value)
                return 0

            lax.fori_loop(0, 16, body, 0)

    def drain(self):
        for way in (0, 1):
            for m in range(self.count):
                self.copy(way, m).wait_send()


def reduce_kernel(
    g_ref, left_ref, right_ref, gm_ref, stat_ref,
    own_a, got_a, own_b, got_b, sum_a, sum_b,
    az_in, az_out, ax_in, ax_out, bx_in, bx_out, bz_in, bz_out,
    az_s, az_r, ax_s, ax_r, bx_s, bx_r, bz_s, bz_r,
    load_a, load_b, swap_a_s, swap_a_r, swap_b_s, swap_b_r, stat_s, stat_r,
):
    x, z, c, y = place()
    partner = device(x, z, 1 - c, y)
    zr, zl = device(x, (z + 1) % NZ, c, y), device(x, (z + NZ - 1) % NZ, c, y)
    xr, xl = device((x + 1) % NX, z, c, y), device((x + NX - 1) % NX, z, c, y)

    barrier = pltpu.get_barrier_semaphore()
    for other in (partner, zr, zl, xr, xl):
        pl.semaphore_signal(barrier, inc=1, device_id=other, device_id_type=MESH)
    pl.semaphore_wait(barrier, 5)

    def slice_a(core, rel):
        start = core * 256 + ((z + rel) % NZ) * 32
        return g_ref.at[0, pl.ds(0, 32), pl.ds(pl.multiple_of(start, 32), 32)]

    def slice_b(core, rel):
        start = core * 256 + ((x + rel) % NX) * 64
        return g_ref.at[0, pl.ds(32, 32), pl.ds(pl.multiple_of(start, 64), 64)]

    def load(kind, rel):
        if kind == "a":
            return pltpu.make_async_copy(slice_a(c, rel), own_a.at[rel], load_a.at[rel])
        return pltpu.make_async_copy(slice_b(c, rel), own_b.at[rel], load_b.at[rel])

    def swap(kind, rel):
        source, target, s, r = (
            (slice_a(1 - c, rel), got_a, swap_a_s, swap_a_r)
            if kind == "a"
            else (slice_b(1 - c, rel), got_b, swap_b_s, swap_b_r)
        )
        return pltpu.make_async_remote_copy(
            src_ref=source, dst_ref=target.at[rel], send_sem=s.at[rel], recv_sem=r.at[rel],
            device_id=partner, device_id_type=MESH,
        )

    order = [("a", 4), ("b", 2), ("a", 3), ("a", 5), ("b", 1), ("b", 3),
             ("a", 2), ("a", 6), ("a", 1), ("a", 7), ("b", 0), ("a", 0)]
    for kind, rel in order:
        swap(kind, rel).start()
        load(kind, rel).start()

    def stat_copy(source):
        return pltpu.make_async_remote_copy(
            src_ref=source.at[0, y % 2], dst_ref=stat_ref, send_sem=stat_s, recv_sem=stat_r,
            device_id=partner, device_id_type=MESH,
        )

    @pl.when(c == 0)
    def _():
        stat_copy(right_ref).start()

    @pl.when(c == 1)
    def _():
        stat_copy(left_ref).start()

    def need(*pieces):
        for kind, rel in pieces:
            load(kind, rel).wait()
            swap(kind, rel).wait_recv()

    def local_az(rel, block):
        return own_a[rel, block].astype(F32) + got_a[rel, block].astype(F32)

    def local_bx(rel, block):
        return own_b[rel, block].astype(F32) + got_b[rel, block].astype(F32)

    def local_ax(rel, block):
        return sum_a[block, pl.ds(pl.multiple_of(((x + rel) % NX) * 8, 8), 8)]

    def local_bz(rel, block):
        return sum_b[block, pl.ds(pl.multiple_of(((z + rel) % NZ) * 8, 8), 8)]

    az = Ring(NZ, zr, zl, az_in, az_out, az_s, az_r, local_az)
    bx = Ring(NX, xr, xl, bx_in, bx_out, bx_s, bx_r, local_bx)
    ax = Ring(NX, xr, xl, ax_in, ax_out, ax_s, ax_r, local_ax)
    bz = Ring(NZ, zr, zl, bz_in, bz_out, bz_s, bz_r, local_bz)

    need(("a", 4))
    az.emit(0)
    need(("b", 2))
    bx.emit(0)
    need(("a", 3), ("a", 5))
    az.emit(1)
    need(("b", 1), ("b", 3))
    bx.emit(1)
    az.emit(2)
    need(("a", 2), ("a", 6))
    az.emit(3)
    bx.emit(2)
    az.emit(4)
    need(("a", 1), ("a", 7))
    az.emit(5)
    az.emit(6)
    need(("b", 0), ("a", 0))

    def store_b(block, value):
        sum_b[block] = value

    def store_a(block, value):
        sum_a[block] = value

    def done_a(block, value):
        gm_ref[block] = value * (1.0 / 64)

    def done_b(block, value):
        gm_ref[32 + block] = value * (1.0 / 64)

    bx.finish(store_b)
    bz.emit(0)
    bz.emit(1)
    bz.emit(2)
    az.finish(store_a)
    ax.emit(0)
    ax.emit(1)
    bz.emit(3)
    bz.emit(4)
    ax.emit(2)
    bz.emit(5)
    bz.emit(6)
    ax.finish(done_a)
    bz.finish(done_b)
    for ring in (az, bx, ax, bz):
        ring.drain()
    for kind, rel in order:
        swap(kind, rel).wait_send()
    stat_copy(left_ref).wait()


def reduce_scatter(grads, left_stats, right_stats):
    vm = pltpu.VMEM
    any_spec = pl.BlockSpec(memory_space=pl.ANY)
    dma = pltpu.SemaphoreType.DMA
    return pl.pallas_call(
        reduce_kernel,
        out_shape=(
            jax.ShapeDtypeStruct((64, 8, 128), F32),
            jax.ShapeDtypeStruct((512, 512), F32),
        ),
        in_specs=[any_spec] * 3,
        out_specs=(pl.BlockSpec(memory_space=pltpu.VMEM), any_spec),
        scratch_shapes=[
            vm((8, 32, 32, 128), BF16), vm((8, 32, 32, 128), BF16),
            vm((4, 32, 64, 128), BF16), vm((4, 32, 64, 128), BF16),
            vm((32, 32, 128), F32), vm((32, 64, 128), F32),
            vm((2, 7, 16, 32, 128), F32), vm((2, 7, 16, 32, 128), F32),
            vm((2, 3, 16, 8, 128), F32), vm((2, 3, 16, 8, 128), F32),
            vm((2, 3, 16, 64, 128), F32), vm((2, 3, 16, 64, 128), F32),
            vm((2, 7, 16, 8, 128), F32), vm((2, 7, 16, 8, 128), F32),
            dma((2, 7)), dma((2, 7)), dma((2, 3)), dma((2, 3)),
            dma((2, 3)), dma((2, 3)), dma((2, 7)), dma((2, 7)),
            dma((8,)), dma((4,)), dma((8,)), dma((8,)), dma((4,)), dma((4,)), dma, dma,
        ],
        compiler_params=pltpu.CompilerParams(
            collective_id=0, has_side_effects=True, vmem_limit_bytes=48 * 1024 * 1024
        ),
        name="reduce_scatter",
    )(grads, left_stats, right_stats)


def split(value):
    high = value.astype(BF16)
    return high, (value - high.astype(F32)).astype(BF16)


def dot(a, b, dims=((1,), (0,))):
    return lax.dot_general(a, b, (dims, ((), ())), preferred_element_type=F32)


def product(a, b, rows, dims=((1,), (0,)), columns=None):
    part = (rows, slice(None)) if columns is None else (slice(None), columns)
    ah, al = a[0][part], a[1][part]
    bh, bl = b[0][...], b[1][...]
    return dot(ah, bh, dims) + (dot(ah, bl, dims) + dot(al, bh, dims))


def diagonal(start, count):
    row = start + lax.broadcasted_iota(jnp.int32, (count, 512), 0)
    return row == lax.broadcasted_iota(jnp.int32, (count, 512), 1)


def tiles(body, count, init=0):
    size = 512 // count

    def step(i, carry):
        start = pl.multiple_of(i * size, size)
        return body(i, start, pl.ds(start, size), carry)

    return lax.fori_loop(0, count, step, init)


def total(value):
    return jnp.sum(jnp.sum(value, axis=0, keepdims=True), axis=1, keepdims=True)


def owner_kernel(
    inv_ref, idx_ref, gm_ref, left_ref, right_ref, stat_ref, out_ref,
    outy, ybuf, hb, g, gh, gl, a, ah, al, a2, sh, sl, fh, fl, th, tl, qh, ql,
    roots, uh, ul, dbuf, rbuf, obuf, fbuf, fin,
    y_s, y_r, x_s, x_r, p_s, p_r, r_s, r_r, b_s, b_r, w_s, w_r, load_sem,
):
    x, z, c, y = place()
    chip = x * NZ + z
    partner = device(x, z, 1 - c, y)

    def far(dx, dz):
        return device((x + dx) % NX, (z + dz) % NZ, c, y)

    rels = [(dx, dz) for dx in range(NX) for dz in range(NZ)]
    barrier = pltpu.get_barrier_semaphore()
    pl.semaphore_signal(barrier, inc=1, device_id=partner, device_id_type=MESH)
    for d in range(1, NY):
        pl.semaphore_signal(barrier, inc=1, device_id=device(x, z, c, (y + d) % NY), device_id_type=MESH)
    for dx, dz in rels[1:]:
        pl.semaphore_signal(barrier, inc=1, device_id=far(dx, dz), device_id_type=MESH)
    pl.semaphore_wait(barrier, 35)

    mine = (y // 2) == c

    def load(source):
        return pltpu.make_async_copy(source, a, load_sem)

    @pl.when(mine & (c == 0))
    def _():
        load(left_ref.at[0, y % 2]).start()

    @pl.when(mine & (c == 1))
    def _():
        load(right_ref.at[0, y % 2]).start()

    @pl.when((y // 2) != c)
    def _():
        load(stat_ref).start()

    def along_y(d, dx):
        xx = (x + dx) % NX
        return pltpu.make_async_remote_copy(
            src_ref=outy.at[d - 1, dx], dst_ref=ybuf.at[y, pl.ds(xx * NZ, NZ)],
            send_sem=y_s.at[d - 1, dx], recv_sem=y_r.at[d - 1, dx],
            device_id=device(x, z, c, (y + d) % NY), device_id_type=MESH,
        )

    for dx in range(NX):
        first = ((x + dx) % NX) * NZ

        def fill(i, _):
            for d in range(1, NY):
                outy[d - 1, dx, i] = gm_ref[inv_ref[(first + i) * 4 + (y + d) % NY]]
            ybuf[y, first + i] = gm_ref[inv_ref[(first + i) * 4 + y]]
            return 0

        lax.fori_loop(0, NZ, fill, 0)
        for d in range(1, NY):
            along_y(d, dx).start()

    def along_xz(dx, dz):
        there = ((x + dx) % NX) * NZ + (z + dz) % NZ
        return pltpu.make_async_remote_copy(
            src_ref=ybuf.at[:, there], dst_ref=hb.at[c, chip],
            send_sem=x_s.at[dx, dz], recv_sem=x_r.at[dx, dz],
            device_id=far(dx, dz), device_id_type=MESH,
        )

    for dx in range(NX):
        for d in range(1, NY):
            along_y(d, dx).wait_recv()
        for dz in range(NZ):
            if dx or dz:
                along_xz(dx, dz).start()
            else:
                hb[c, chip] = ybuf[:, chip]

    def across(dx):
        part = hb.at[c, pl.ds(((x + NX - dx) % NX) * NZ, NZ)]
        return pltpu.make_async_remote_copy(
            src_ref=part, dst_ref=part, send_sem=p_s.at[dx], recv_sem=p_r.at[dx],
            device_id=partner, device_id_type=MESH,
        )

    for dx in range(NX):
        for dz in range(NZ):
            if dx or dz:
                along_xz(dx, dz).wait_recv()
        across(dx).start()
    for dx in range(NX):
        across(dx).wait()

    early = inv_ref[chip * 4 + y] < 32

    def assemble(p, _):
        piece = jnp.where(early, (p % NX) * NZ + p // NX, p)
        for core in range(2):
            start = pl.multiple_of(core * 256 + p * 8, 8)
            for yy in range(NY):
                g[pl.ds(start, 8), yy * 128:yy * 128 + 128] = hb[core, piece, yy]
        return 0

    lax.fori_loop(0, 32, assemble, 0)

    def split_g(i, start, rows, squares):
        value = g[rows, :]
        gh[rows, :], gl[rows, :] = split(value)
        return squares + total(value * value)

    zero = jnp.zeros((1, 1), F32)
    grad_squares = tiles(split_g, 8, zero)

    load(stat_ref).wait()
    pair_g = (gh, gl)

    def rows_of(i):
        return pl.ds(i * 256, 256)

    @pl.when(c == 0)
    def _():
        for i in range(2):
            a[rows_of(i), :] = 0.95 * a[rows_of(i), :] + product(pair_g, pair_g, rows_of(i), ((1,), (1,)))

    @pl.when(c == 1)
    def _():
        for i in range(2):
            a[rows_of(i), :] = 0.95 * a[rows_of(i), :] + product(
                pair_g, pair_g, None, ((0,), (0,)), columns=rows_of(i)
            )

    def trace_of(i, start, rows, trace):
        return trace + total(jnp.where(diagonal(start, 64), a[rows, :], 0.0))

    size = tiles(trace_of, 8, zero) * (1.0 / 512)
    scale = 1.0 / size

    def split_a(i, start, rows, carry):
        value = a[rows, :] * scale
        a[rows, :] = value
        ah[rows, :], al[rows, :] = split(value)
        return carry

    tiles(split_a, 8)
    pair_a = (ah, al)

    def square(i, start, rows, carry):
        a2[rows, :] = product(pair_a, pair_a, rows)
        return carry

    tiles(square, 2)

    def unit(image):
        return image / jnp.sqrt(total(image * image))

    vector = jnp.full((1, 512), 512 ** (-0.5), F32)
    vector = unit(jnp.sum(a2[...] * vector, axis=1, keepdims=True))
    vector = unit(jnp.sum(a2[...] * vector, axis=0, keepdims=True))
    vector = unit(jnp.sum(a2[...] * vector, axis=1, keepdims=True))
    image = jnp.sum(a[...] * vector, axis=0, keepdims=True)
    flat = jnp.sum(jnp.where(diagonal(0, 512), vector, 0.0), axis=0, keepdims=True)
    largest = total(flat * image)
    factor = 2.5 / largest
    fourth = jnp.sqrt(jnp.sqrt(factor * scale))

    def first_terms(i, start, rows, carry):
        eye = jnp.where(diagonal(start, 64), 1.0, 0.0)
        value = a[rows, :] * factor
        qh[rows, :], ql[rows, :] = split(1.25 * eye - 0.25 * value)
        squared = (25.0 / 16) * eye - (10.0 / 16) * value + (factor * factor * (1.0 / 16)) * a2[rows, :]
        sh[rows, :], sl[rows, :] = split(squared)
        return carry

    tiles(first_terms, 8)

    def power_four(i, start, rows, carry):
        fh[rows, :], fl[rows, :] = split(product((sh, sl), (sh, sl), rows))
        return carry

    tiles(power_four, 2)

    def second_term(i, start, rows, carry):
        value = product((fh, fl), pair_a, rows) * (0.25 * factor)
        th[rows, :], tl[rows, :] = split(jnp.where(diagonal(start, 256), 1.25, 0.0) - value)
        return carry

    tiles(second_term, 2)

    def send_root(i):
        part = roots.at[c, :, pl.ds(i * 256, 256)]
        return pltpu.make_async_remote_copy(
            src_ref=part, dst_ref=part, send_sem=r_s.at[i], recv_sem=r_r.at[i],
            device_id=partner, device_id_type=MESH,
        )

    for i in range(2):
        rows = rows_of(i)
        high, low = split(product((qh, ql), (th, tl), rows) * fourth)
        roots[c, 0, rows, :] = high
        roots[c, 1, rows, :] = low
        send_root(i).start()

    pair_l = (roots.at[0, 0], roots.at[0, 1])
    pair_r = (roots.at[1, 0], roots.at[1, 1])
    pair_u = (uh, ul)

    def middle(one, two):
        def body(i, start, rows, carry):
            uh[rows, :], ul[rows, :] = split(product(one, two, rows))
            return carry

        tiles(body, 2)

    @pl.when(c == 0)
    def _():
        middle(pair_l, pair_g)

    @pl.when(c == 1)
    def _():
        middle(pair_g, pair_r)

    for i in range(2):
        send_root(i).wait_recv()

    def outer(one, two):
        def body(i, start, rows, carry):
            a2[rows, :] = product(one, two, rows)
            return carry

        tiles(body, 2)

    @pl.when(c == 0)
    def _():
        outer(pair_u, pair_r)

    @pl.when(c == 1)
    def _():
        outer(pair_l, pair_u)

    def squares_of(i, start, rows, carry):
        value = a2[rows, :]
        return carry + total(value * value)

    ratio = jnp.sqrt((grad_squares + 1e-06) / (tiles(squares_of, 8, zero) + 1e-06))

    def bands(q, _):
        rows = a2[pl.ds(pl.multiple_of(q * 16 + c * 8, 8), 8), :] * ratio
        dbuf[q] = jnp.concatenate([rows[:, :256], rows[:, 256:]], axis=0).astype(BF16)
        return 0

    lax.fori_loop(0, 32, bands, 0)

    def back_xz(dx, dz):
        there = ((x + dx) % NX) * NZ + (z + dz) % NZ
        return pltpu.make_async_remote_copy(
            src_ref=dbuf.at[there], dst_ref=rbuf.at[chip],
            send_sem=b_s.at[dx, dz], recv_sem=b_r.at[dx, dz],
            device_id=far(dx, dz), device_id_type=MESH,
        )

    for dx, dz in rels[1:]:
        back_xz(dx, dz).start()
    rbuf[chip] = dbuf[chip]
    for dx, dz in rels[1:]:
        back_xz(dx, dz).wait_recv()

    def regroup(t, _):
        one, two = rbuf[2 * t].astype(F32), rbuf[2 * t + 1].astype(F32)
        for yy in range(NY):
            low, left = (yy // 2) * 8, (yy % 2) * 128
            pair = [v[low:low + 8, left:left + 128] for v in (one, two)]
            obuf[yy, t] = jnp.concatenate(pair, axis=0).astype(BF16)
        return 0

    lax.fori_loop(0, 16, regroup, 0)

    def back_y(d):
        return pltpu.make_async_remote_copy(
            src_ref=obuf.at[(y + d) % NY], dst_ref=fbuf.at[y],
            send_sem=w_s.at[d - 1], recv_sem=w_r.at[d - 1],
            device_id=device(x, z, c, (y + d) % NY), device_id_type=MESH,
        )

    for d in range(1, NY):
        back_y(d).start()
    fbuf[y] = obuf[y]
    for d in range(1, NY):
        back_y(d).wait_recv()

    def unpack(t, _):
        for yy in range(NY):
            pair = fbuf[yy, t].astype(F32)
            fin[yy * 32 + 2 * t] = pair[:8]
            fin[yy * 32 + 2 * t + 1] = pair[8:]
        return 0

    lax.fori_loop(0, 16, unpack, 0)

    def pick(k, _):
        out_ref[k] = fin[idx_ref[k]].astype(BF16)
        return 0

    lax.fori_loop(0, 64, pick, 0)

    for dx in range(NX):
        for d in range(1, NY):
            along_y(d, dx).wait_send()
    for dx, dz in rels[1:]:
        along_xz(dx, dz).wait_send()
        back_xz(dx, dz).wait_send()
    for i in range(2):
        send_root(i).wait_send()
    for d in range(1, NY):
        back_y(d).wait_send()


def owner_step(inv, idx, gmean, left_stats, right_stats, stat):
    vm = pltpu.VMEM
    any_spec = pl.BlockSpec(memory_space=pl.ANY)
    smem = pl.BlockSpec(memory_space=pltpu.SMEM)
    vmem = pl.BlockSpec(memory_space=pltpu.VMEM)
    dma = pltpu.SemaphoreType.DMA
    full, half = vm((512, 512), F32), vm((512, 512), BF16)
    return pl.pallas_call(
        owner_kernel,
        out_shape=jax.ShapeDtypeStruct((64, 8, 128), BF16),
        in_specs=[smem, smem, vmem, any_spec, any_spec, any_spec],
        out_specs=vmem,
        scratch_shapes=[
            vm((3, 4, 8, 8, 128), F32), vm((4, 32, 8, 128), F32), vm((2, 32, 4, 8, 128), F32),
            full, half, half, full, half, half, full,
            half, half, half, half, half, half, half, half,
            vm((2, 2, 512, 512), BF16), half, half,
            vm((32, 16, 256), BF16), vm((32, 16, 256), BF16),
            vm((4, 16, 16, 128), BF16), vm((4, 16, 16, 128), BF16), vm((128, 8, 128), F32),
            dma((3, 4)), dma((3, 4)), dma((4, 8)), dma((4, 8)), dma((4,)), dma((4,)),
            dma((2,)), dma((2,)), dma((4, 8)), dma((4, 8)), dma((3,)), dma((3,)), dma,
        ],
        compiler_params=pltpu.CompilerParams(
            collective_id=1, has_side_effects=True, vmem_limit_bytes=40 * 1024 * 1024
        ),
        name="owner_step",
    )(inv, idx, gmean, left_stats, right_stats, stat)


def shards(grads, left_stats, right_stats, owners, slots):
    place_of = owners * CAP + slots
    hit = place_of[None, :] == jnp.arange(128, dtype=jnp.int32)[:, None]
    inv = jnp.sum(jnp.where(hit, jnp.arange(64, dtype=jnp.int32)[None, :], 0), axis=1)
    idx = (place_of % 4) * 32 + place_of // 4
    gmean, stat = reduce_scatter(grads, left_stats, right_stats)
    return owner_step(inv, idx, gmean, left_stats, right_stats, stat)


def solution(mesh):
    in_specs = (
        P("dp", None, None, "mp"),
        P("dp", None, None, None),
        P("dp", None, None, None),
        P(),
        P(),
    )
    out_specs = P(None, "dp", "mp")
    return jax.shard_map(shards, mesh=mesh, in_specs=in_specs, out_specs=out_specs, check_vma=False)
```

```python
import jax
import jax.numpy as jnp
from jax import lax
from jax.experimental import pallas as pl
from jax.experimental.pallas import tpu as pltpu
from jax.sharding import PartitionSpec as P

CAP = 2
NX, NZ, NY = 4, 8, 4
MESH = pl.DeviceIdType.MESH
F32 = jnp.float32
BF16 = jnp.bfloat16
I16 = jnp.int16


def place():
    dp = lax.axis_index("dp")
    chip = dp // 2
    return chip // NZ, chip % NZ, dp % 2, lax.axis_index("mp")


def device(x, z, c, y):
    return ((x * NZ + z) * 2 + c, y)


class Ring:
    def __init__(self, n, r, right, left, inbox, outbox, send, recv, local, work):
        self.n, self.r, self.to = n, r, (right, left)
        self.inbox, self.outbox, self.send, self.recv, self.local = inbox, outbox, send, recv, local
        self.stage, self.peak, self.scale = work
        self.count = n - 1
        self.group = 128 // r
        self.groups = 16 // self.group

    def copy(self, way, m):
        return pltpu.make_async_remote_copy(
            src_ref=self.outbox.at[way, m],
            dst_ref=self.inbox.at[way, m],
            send_sem=self.send.at[way, m],
            recv_sem=self.recv.at[way, m],
            device_id=self.to[way],
            device_id_type=MESH,
        )

    def open(self, way, m, slot):
        steps = self.inbox[way, m, pl.ds(16 * self.r, 16), :].astype(jnp.int32).astype(F32)
        self.scale[slot] = jnp.exp(steps * (1.0 / 128)) * (1.0 / 32760)

    def spread(self, i, slot):
        rows = [self.scale[slot, pl.ds(i * self.group + q, 1), :] for q in range(self.group)]
        return jnp.concatenate([jnp.broadcast_to(row, (self.r, 128)) for row in rows], axis=0)

    def taken(self, way, m, i, slot):
        data = self.inbox[way, m, pl.ds(pl.multiple_of(i * 128, 128), 128), :]
        return data.astype(jnp.int32).astype(F32) * self.spread(i, slot)

    def own(self, step, half, i):
        return self.local(step, half * 16 + i * self.group, self.group).reshape(128, 128)

    def emit(self, m):
        hops = self.n // 2 - (m + 1) // 2
        for way in (0, 1):
            half = way if m % 2 == 0 else 1 - way
            step = hops if way == 0 else self.n - hops
            if m >= 2:
                self.copy(way, m - 2).wait_recv()
                self.open(way, m - 2, 0)

            def add(i, _):
                value = self.own(step, half, i)
                if m >= 2:
                    value = value + self.taken(way, m - 2, i, 0)
                self.stage[pl.ds(pl.multiple_of(i * 128, 128), 128), :] = value
                size = jnp.abs(value)
                for q in range(self.group):
                    self.peak[pl.ds(i * self.group + q, 1), :] = jnp.max(
                        size[q * self.r:(q + 1) * self.r], axis=0, keepdims=True
                    )
                return 0

            lax.fori_loop(0, self.groups, add, 0)
            steps = jnp.ceil(jnp.log(jnp.maximum(self.peak[...], 1e-30)) * 128)
            self.scale[1] = jnp.exp(steps * (-1.0 / 128)) * 32760
            self.outbox[way, m, pl.ds(16 * self.r, 16), :] = steps.astype(jnp.int32).astype(I16)

            def code(i, _):
                rows = pl.ds(pl.multiple_of(i * 128, 128), 128)
                value = jnp.round(self.stage[rows, :] * self.spread(i, 1))
                self.outbox[way, m, rows, :] = value.astype(jnp.int32).astype(I16)
                return 0

            lax.fori_loop(0, self.groups, code, 0)
            self.copy(way, m).start()

    def finish(self, store):
        last = self.count - 1
        for half in (0, 1):
            first = last if half == 0 else last - 1
            second = last - 1 if half == 0 else last
            self.copy(0, first).wait_recv()
            self.copy(1, second).wait_recv()
            self.open(0, first, 0)
            self.open(1, second, 1)

            def body(i, _):
                value = self.own(0, half, i)
                value = value + self.taken(0, first, i, 0) + self.taken(1, second, i, 1)
                store(half * 16 + i * self.group, value.reshape(self.group, self.r, 128))
                return 0

            lax.fori_loop(0, self.groups, body, 0)

    def drain(self):
        for way in (0, 1):
            for m in range(self.count):
                self.copy(way, m).wait_send()


def reduce_part(
    g_ref, left_ref, right_ref, gm_ref, a,
    stage, peak, scale, own_a, got_a, own_b, got_b, sum_a, sum_b,
    az_in, az_out, ax_in, ax_out, bx_in, bx_out, bz_in, bz_out,
    az_s, az_r, ax_s, ax_r, bx_s, bx_r, bz_s, bz_r,
    load_a, load_b, swap_a_s, swap_a_r, swap_b_s, swap_b_r, stat_s, stat_r, load_sem,
):
    x, z, c, y = place()
    partner = device(x, z, 1 - c, y)
    zr, zl = device(x, (z + 1) % NZ, c, y), device(x, (z + NZ - 1) % NZ, c, y)
    xr, xl = device((x + 1) % NX, z, c, y), device((x + NX - 1) % NX, z, c, y)

    def slice_a(core, rel):
        start = core * 256 + ((z + rel) % NZ) * 32
        return g_ref.at[0, pl.ds(0, 32), pl.ds(pl.multiple_of(start, 32), 32)]

    def slice_b(core, rel):
        start = core * 256 + ((x + rel) % NX) * 64
        return g_ref.at[0, pl.ds(32, 32), pl.ds(pl.multiple_of(start, 64), 64)]

    def load(kind, rel):
        if kind == "a":
            return pltpu.make_async_copy(slice_a(c, rel), own_a.at[rel], load_a.at[rel])
        return pltpu.make_async_copy(slice_b(c, rel), own_b.at[rel], load_b.at[rel])

    def swap(kind, rel):
        source, target, s, r = (
            (slice_a(1 - c, rel), got_a, swap_a_s, swap_a_r)
            if kind == "a"
            else (slice_b(1 - c, rel), got_b, swap_b_s, swap_b_r)
        )
        return pltpu.make_async_remote_copy(
            src_ref=source, dst_ref=target.at[rel], send_sem=s.at[rel], recv_sem=r.at[rel],
            device_id=partner, device_id_type=MESH,
        )

    order = [("a", 4), ("b", 2), ("a", 3), ("a", 5), ("b", 1), ("b", 3),
             ("a", 2), ("a", 6), ("a", 1), ("a", 7), ("b", 0), ("a", 0)]
    for kind, rel in order:
        swap(kind, rel).start()
        load(kind, rel).start()

    mine = (y // 2) == c

    def keep(source):
        return pltpu.make_async_copy(source.at[0, y % 2], a, load_sem)

    def give(source):
        return pltpu.make_async_remote_copy(
            src_ref=source.at[0, y % 2], dst_ref=a, send_sem=stat_s, recv_sem=stat_r,
            device_id=partner, device_id_type=MESH,
        )

    @pl.when(mine & (c == 0))
    def _():
        keep(left_ref).start()
        give(right_ref).start()

    @pl.when(mine & (c == 1))
    def _():
        keep(right_ref).start()
        give(left_ref).start()

    def need(*pieces):
        for kind, rel in pieces:
            load(kind, rel).wait()
            swap(kind, rel).wait_recv()

    def local_az(rel, block, count):
        blocks = pl.ds(block, count)
        return own_a[rel, blocks].astype(F32) + got_a[rel, blocks].astype(F32)

    def local_bx(rel, block, count):
        blocks = pl.ds(block, count)
        return own_b[rel, blocks].astype(F32) + got_b[rel, blocks].astype(F32)

    def local_ax(rel, block, count):
        return sum_a[pl.ds(block, count), pl.ds(pl.multiple_of(((x + rel) % NX) * 8, 8), 8)]

    def local_bz(rel, block, count):
        return sum_b[pl.ds(block, count), pl.ds(pl.multiple_of(((z + rel) % NZ) * 8, 8), 8)]

    work = (stage, peak, scale)
    az = Ring(NZ, 32, zr, zl, az_in, az_out, az_s, az_r, local_az, work)
    bx = Ring(NX, 64, xr, xl, bx_in, bx_out, bx_s, bx_r, local_bx, work)
    ax = Ring(NX, 8, xr, xl, ax_in, ax_out, ax_s, ax_r, local_ax, work)
    bz = Ring(NZ, 8, zr, zl, bz_in, bz_out, bz_s, bz_r, local_bz, work)

    need(("a", 4))
    az.emit(0)
    need(("b", 2))
    bx.emit(0)
    need(("a", 3), ("a", 5))
    az.emit(1)
    need(("b", 1), ("b", 3))
    bx.emit(1)
    az.emit(2)
    need(("a", 2), ("a", 6))
    az.emit(3)
    bx.emit(2)
    az.emit(4)
    need(("a", 1), ("a", 7))
    az.emit(5)
    az.emit(6)
    need(("b", 0), ("a", 0))

    def store_b(block, value):
        sum_b[pl.ds(block, 2)] = value

    def store_a(block, value):
        sum_a[pl.ds(block, 4)] = value

    def done_a(block, value):
        gm_ref[pl.ds(block, 16)] = value * (1.0 / 64)

    def done_b(block, value):
        gm_ref[pl.ds(32 + block, 16)] = value * (1.0 / 64)

    bx.finish(store_b)
    bz.emit(0)
    bz.emit(1)
    bz.emit(2)
    az.finish(store_a)
    ax.emit(0)
    ax.emit(1)
    bz.emit(3)
    bz.emit(4)
    ax.emit(2)
    bz.emit(5)
    bz.emit(6)
    ax.finish(done_a)
    bz.finish(done_b)
    for ring in (az, bx, ax, bz):
        ring.drain()
    for kind, rel in order:
        swap(kind, rel).wait_send()

    @pl.when(mine)
    def _():
        keep(left_ref).wait()
        give(left_ref).wait_send()

    @pl.when((y // 2) != c)
    def _():
        give(left_ref).wait_recv()


def split(value):
    high = value.astype(BF16)
    return high, (value - high.astype(F32)).astype(BF16)


def dot(a, b, dims=((1,), (0,))):
    return lax.dot_general(a, b, (dims, ((), ())), preferred_element_type=F32)


def product(a, b, rows, dims=((1,), (0,)), columns=None):
    part = (rows, slice(None)) if columns is None else (slice(None), columns)
    ah, al = a[0][part], a[1][part]
    bh, bl = b[0][...], b[1][...]
    return dot(ah, bh, dims) + (dot(ah, bl, dims) + dot(al, bh, dims))


def diagonal(start, count):
    row = start + lax.broadcasted_iota(jnp.int32, (count, 512), 0)
    return row == lax.broadcasted_iota(jnp.int32, (count, 512), 1)


def tiles(body, count, init=0):
    size = 512 // count

    def step(i, carry):
        start = pl.multiple_of(i * size, size)
        return body(i, start, pl.ds(start, size), carry)

    return lax.fori_loop(0, count, step, init)


def total(value):
    return jnp.sum(jnp.sum(value, axis=0, keepdims=True), axis=1, keepdims=True)


def owner_part(
    inv_ref, idx_ref, gm_ref, a, out_ref,
    outy, ybuf, hb, g, gh, gl, ah, al, a2, sh, sl, fh, fl, th, tl, qh, ql,
    roots, uh, ul, dbuf, rbuf, obuf, fbuf, fin,
    y_s, y_r, x_s, x_r, p_s, p_r, r_s, r_r, b_s, b_r, w_s, w_r,
):
    x, z, c, y = place()
    chip = x * NZ + z
    partner = device(x, z, 1 - c, y)

    def far(dx, dz):
        return device((x + dx) % NX, (z + dz) % NZ, c, y)

    rels = [(dx, dz) for dx in range(NX) for dz in range(NZ)]
    def along_y(d, dx):
        xx = (x + dx) % NX
        return pltpu.make_async_remote_copy(
            src_ref=outy.at[d - 1, dx], dst_ref=ybuf.at[y, pl.ds(xx * NZ, NZ)],
            send_sem=y_s.at[d - 1, dx], recv_sem=y_r.at[d - 1, dx],
            device_id=device(x, z, c, (y + d) % NY), device_id_type=MESH,
        )

    for dx in range(NX):
        first = ((x + dx) % NX) * NZ

        def fill(i, _):
            for d in range(1, NY):
                outy[d - 1, dx, i] = gm_ref[inv_ref[(first + i) * 4 + (y + d) % NY]]
            ybuf[y, first + i] = gm_ref[inv_ref[(first + i) * 4 + y]]
            return 0

        lax.fori_loop(0, NZ, fill, 0)
        for d in range(1, NY):
            along_y(d, dx).start()

    def along_xz(dx, dz):
        there = ((x + dx) % NX) * NZ + (z + dz) % NZ
        return pltpu.make_async_remote_copy(
            src_ref=ybuf.at[:, there], dst_ref=hb.at[c, chip],
            send_sem=x_s.at[dx, dz], recv_sem=x_r.at[dx, dz],
            device_id=far(dx, dz), device_id_type=MESH,
        )

    for dx in range(NX):
        for d in range(1, NY):
            along_y(d, dx).wait_recv()
        for dz in range(NZ):
            if dx or dz:
                along_xz(dx, dz).start()
            else:
                hb[c, chip] = ybuf[:, chip]

    def across(dx):
        part = hb.at[c, pl.ds(((x + NX - dx) % NX) * NZ, NZ)]
        return pltpu.make_async_remote_copy(
            src_ref=part, dst_ref=part, send_sem=p_s.at[dx], recv_sem=p_r.at[dx],
            device_id=partner, device_id_type=MESH,
        )

    for dx in range(NX):
        for dz in range(NZ):
            if dx or dz:
                along_xz(dx, dz).wait_recv()
        across(dx).start()
    for dx in range(NX):
        across(dx).wait()

    early = inv_ref[chip * 4 + y] < 32

    def assemble(p, _):
        piece = jnp.where(early, (p % NX) * NZ + p // NX, p)
        for core in range(2):
            start = pl.multiple_of(core * 256 + p * 8, 8)
            for yy in range(NY):
                g[pl.ds(start, 8), yy * 128:yy * 128 + 128] = hb[core, piece, yy]
        return 0

    lax.fori_loop(0, 32, assemble, 0)

    def split_g(i, start, rows, squares):
        value = g[rows, :]
        gh[rows, :], gl[rows, :] = split(value)
        return squares + total(value * value)

    zero = jnp.zeros((1, 1), F32)
    grad_squares = tiles(split_g, 8, zero)

    pair_g = (gh, gl)

    def rows_of(i):
        return pl.ds(i * 256, 256)

    @pl.when(c == 0)
    def _():
        for i in range(2):
            a[rows_of(i), :] = 0.95 * a[rows_of(i), :] + product(pair_g, pair_g, rows_of(i), ((1,), (1,)))

    @pl.when(c == 1)
    def _():
        for i in range(2):
            a[rows_of(i), :] = 0.95 * a[rows_of(i), :] + product(
                pair_g, pair_g, None, ((0,), (0,)), columns=rows_of(i)
            )

    def trace_of(i, start, rows, trace):
        return trace + total(jnp.where(diagonal(start, 64), a[rows, :], 0.0))

    size = tiles(trace_of, 8, zero) * (1.0 / 512)
    scale = 1.0 / size

    def split_a(i, start, rows, carry):
        value = a[rows, :] * scale
        a[rows, :] = value
        ah[rows, :], al[rows, :] = split(value)
        return carry

    tiles(split_a, 8)
    pair_a = (ah, al)

    def square(i, start, rows, carry):
        a2[rows, :] = product(pair_a, pair_a, rows)
        return carry

    tiles(square, 2)

    def unit(image):
        return image / jnp.sqrt(total(image * image))

    vector = jnp.full((1, 512), 512 ** (-0.5), F32)
    vector = unit(jnp.sum(a2[...] * vector, axis=1, keepdims=True))
    vector = unit(jnp.sum(a2[...] * vector, axis=0, keepdims=True))
    vector = unit(jnp.sum(a2[...] * vector, axis=1, keepdims=True))
    image = jnp.sum(a[...] * vector, axis=0, keepdims=True)
    flat = jnp.sum(jnp.where(diagonal(0, 512), vector, 0.0), axis=0, keepdims=True)
    largest = total(flat * image)
    factor = 2.5 / largest
    fourth = jnp.sqrt(jnp.sqrt(factor * scale))

    def first_terms(i, start, rows, carry):
        eye = jnp.where(diagonal(start, 64), 1.0, 0.0)
        value = a[rows, :] * factor
        qh[rows, :], ql[rows, :] = split(1.25 * eye - 0.25 * value)
        squared = (25.0 / 16) * eye - (10.0 / 16) * value + (factor * factor * (1.0 / 16)) * a2[rows, :]
        sh[rows, :], sl[rows, :] = split(squared)
        return carry

    tiles(first_terms, 8)

    def power_four(i, start, rows, carry):
        fh[rows, :], fl[rows, :] = split(product((sh, sl), (sh, sl), rows))
        return carry

    tiles(power_four, 2)

    def second_term(i, start, rows, carry):
        value = product((fh, fl), pair_a, rows) * (0.25 * factor)
        th[rows, :], tl[rows, :] = split(jnp.where(diagonal(start, 256), 1.25, 0.0) - value)
        return carry

    tiles(second_term, 2)

    def send_root(i):
        part = roots.at[c, :, pl.ds(i * 256, 256)]
        return pltpu.make_async_remote_copy(
            src_ref=part, dst_ref=part, send_sem=r_s.at[i], recv_sem=r_r.at[i],
            device_id=partner, device_id_type=MESH,
        )

    for i in range(2):
        rows = rows_of(i)
        high, low = split(product((qh, ql), (th, tl), rows) * fourth)
        roots[c, 0, rows, :] = high
        roots[c, 1, rows, :] = low
        send_root(i).start()

    pair_l = (roots.at[0, 0], roots.at[0, 1])
    pair_r = (roots.at[1, 0], roots.at[1, 1])
    pair_u = (uh, ul)

    def middle(one, two):
        def body(i, start, rows, carry):
            uh[rows, :], ul[rows, :] = split(product(one, two, rows))
            return carry

        tiles(body, 2)

    @pl.when(c == 0)
    def _():
        middle(pair_l, pair_g)

    @pl.when(c == 1)
    def _():
        middle(pair_g, pair_r)

    for i in range(2):
        send_root(i).wait_recv()

    def outer(one, two):
        def body(i, start, rows, carry):
            a2[rows, :] = product(one, two, rows)
            return carry

        tiles(body, 2)

    @pl.when(c == 0)
    def _():
        outer(pair_u, pair_r)

    @pl.when(c == 1)
    def _():
        outer(pair_l, pair_u)

    def squares_of(i, start, rows, carry):
        value = a2[rows, :]
        return carry + total(value * value)

    ratio = jnp.sqrt((grad_squares + 1e-06) / (tiles(squares_of, 8, zero) + 1e-06))

    def bands(q, _):
        rows = a2[pl.ds(pl.multiple_of(q * 16 + c * 8, 8), 8), :] * ratio
        dbuf[q] = jnp.concatenate([rows[:, :256], rows[:, 256:]], axis=0).astype(BF16)
        return 0

    lax.fori_loop(0, 32, bands, 0)

    def back_xz(dx, dz):
        there = ((x + dx) % NX) * NZ + (z + dz) % NZ
        return pltpu.make_async_remote_copy(
            src_ref=dbuf.at[there], dst_ref=rbuf.at[chip],
            send_sem=b_s.at[dx, dz], recv_sem=b_r.at[dx, dz],
            device_id=far(dx, dz), device_id_type=MESH,
        )

    for dx, dz in rels[1:]:
        back_xz(dx, dz).start()
    rbuf[chip] = dbuf[chip]
    for dx, dz in rels[1:]:
        back_xz(dx, dz).wait_recv()

    def regroup(t, _):
        one, two = rbuf[2 * t].astype(F32), rbuf[2 * t + 1].astype(F32)
        for yy in range(NY):
            low, left = (yy // 2) * 8, (yy % 2) * 128
            pair = [v[low:low + 8, left:left + 128] for v in (one, two)]
            obuf[yy, t] = jnp.concatenate(pair, axis=0).astype(BF16)
        return 0

    lax.fori_loop(0, 16, regroup, 0)

    def back_y(d):
        return pltpu.make_async_remote_copy(
            src_ref=obuf.at[(y + d) % NY], dst_ref=fbuf.at[y],
            send_sem=w_s.at[d - 1], recv_sem=w_r.at[d - 1],
            device_id=device(x, z, c, (y + d) % NY), device_id_type=MESH,
        )

    for d in range(1, NY):
        back_y(d).start()
    fbuf[y] = obuf[y]
    for d in range(1, NY):
        back_y(d).wait_recv()

    def unpack(t, _):
        for yy in range(NY):
            pair = fbuf[yy, t].astype(F32)
            fin[yy * 32 + 2 * t] = pair[:8]
            fin[yy * 32 + 2 * t + 1] = pair[8:]
        return 0

    lax.fori_loop(0, 16, unpack, 0)

    def pick(k, _):
        out_ref[k] = fin[idx_ref[k]].astype(BF16)
        return 0

    lax.fori_loop(0, 64, pick, 0)

    for dx in range(NX):
        for d in range(1, NY):
            along_y(d, dx).wait_send()
    for dx, dz in rels[1:]:
        along_xz(dx, dz).wait_send()
        back_xz(dx, dz).wait_send()
    for i in range(2):
        send_root(i).wait_send()
    for d in range(1, NY):
        back_y(d).wait_send()


OWNER_SCRATCH = 37


def kernel(inv_ref, idx_ref, g_ref, left_ref, right_ref, out_ref, gm, a, *scratch):
    x, z, c, y = place()
    others = [device(x, z, 1 - c, y)]
    others += [device(x, z, c, (y + d) % NY) for d in range(1, NY)]
    others += [
        device((x + dx) % NX, (z + dz) % NZ, c, y) for dx in range(NX) for dz in range(NZ) if dx or dz
    ]
    barrier = pltpu.get_barrier_semaphore()
    for other in others:
        pl.semaphore_signal(barrier, inc=1, device_id=other, device_id_type=MESH)
    pl.semaphore_wait(barrier, len(others))
    ring = len(scratch) - OWNER_SCRATCH
    reduce_part(g_ref, left_ref, right_ref, gm, a, *scratch[:ring])
    owner_part(inv_ref, idx_ref, gm, a, out_ref, *scratch[ring:])


def step(inv, idx, grads, left_stats, right_stats):
    vm = pltpu.VMEM
    dma = pltpu.SemaphoreType.DMA
    hbm = pl.BlockSpec(memory_space=pltpu.HBM)
    smem = pl.BlockSpec(memory_space=pltpu.SMEM)
    full, half = vm((512, 512), F32), vm((512, 512), BF16)

    def boxes(count, r):
        return [vm((2, count, 16 * r + 16, 128), I16)] * 2

    ring = [
        vm((1024, 128), F32), vm((16, 128), F32), vm((2, 16, 128), F32),
        vm((8, 32, 32, 128), BF16), vm((8, 32, 32, 128), BF16),
        vm((4, 32, 64, 128), BF16), vm((4, 32, 64, 128), BF16),
        vm((32, 32, 128), F32), vm((32, 64, 128), F32),
        *boxes(7, 32), *boxes(3, 8), *boxes(3, 64), *boxes(7, 8),
        dma((2, 7)), dma((2, 7)), dma((2, 3)), dma((2, 3)),
        dma((2, 3)), dma((2, 3)), dma((2, 7)), dma((2, 7)),
        dma((8,)), dma((4,)), dma((8,)), dma((8,)), dma((4,)), dma((4,)), dma, dma, dma,
    ]
    owner = [
        vm((3, 4, 8, 8, 128), F32), vm((4, 32, 8, 128), F32), vm((2, 32, 4, 8, 128), F32),
        full, half, half, half, half, full,
        half, half, half, half, half, half, half, half,
        vm((2, 2, 512, 512), BF16), half, half,
        vm((32, 16, 256), BF16), vm((32, 16, 256), BF16),
        vm((4, 16, 16, 128), BF16), vm((4, 16, 16, 128), BF16), vm((128, 8, 128), F32),
        dma((3, 4)), dma((3, 4)), dma((4, 8)), dma((4, 8)), dma((4,)), dma((4,)),
        dma((2,)), dma((2,)), dma((4, 8)), dma((4, 8)), dma((3,)), dma((3,)),
    ]
    assert len(owner) == OWNER_SCRATCH
    return pl.pallas_call(
        kernel,
        out_shape=jax.ShapeDtypeStruct((64, 8, 128), BF16),
        in_specs=[smem, smem, hbm, hbm, hbm],
        out_specs=pl.BlockSpec(memory_space=pltpu.VMEM),
        scratch_shapes=[vm((64, 8, 128), F32), full, *ring, *owner],
        compiler_params=pltpu.CompilerParams(
            collective_id=0, has_side_effects=True, vmem_limit_bytes=56 * 1024 * 1024
        ),
        name="shampoo_step",
    )(inv, idx, grads, left_stats, right_stats)


def shards(grads, left_stats, right_stats, owners, slots):
    place_of = owners * CAP + slots
    hit = place_of[None, :] == jnp.arange(128, dtype=jnp.int32)[:, None]
    inv = jnp.sum(jnp.where(hit, jnp.arange(64, dtype=jnp.int32)[None, :], 0), axis=1)
    idx = (place_of % 4) * 32 + place_of // 4
    return step(inv, idx, grads, left_stats, right_stats)


def solution(mesh):
    in_specs = (
        P("dp", None, None, "mp"),
        P("dp", None, None, None),
        P("dp", None, None, None),
        P(),
        P(),
    )
    out_specs = P(None, "dp", "mp")
    return jax.shard_map(shards, mesh=mesh, in_specs=in_specs, out_specs=out_specs, check_vma=False)
```

```python
import jax
import jax.numpy as jnp
from jax import lax
from jax.experimental import pallas as pl
from jax.experimental.pallas import tpu as pltpu
from jax.sharding import PartitionSpec as P

CAP = 2
NX, NZ, NY = 4, 8, 4
AHEAD = 5
FORWARD = ((4, 5, 3, 6), (2, 7, 1, 0))
BACK = ((4, 5, 3, 6), (2, 7, 1, 0))
MESH = pl.DeviceIdType.MESH
F32 = jnp.float32
BF16 = jnp.bfloat16
I16 = jnp.int16


def place():
    dp = lax.axis_index("dp")
    chip = dp // 2
    return chip // NZ, chip % NZ, dp % 2, lax.axis_index("mp")


def device(x, z, c, y):
    return ((x * NZ + z) * 2 + c, y)


class Ring:
    def __init__(self, n, r, right, left, inbox, outbox, send, recv, local, work):
        self.n, self.r, self.to = n, r, (right, left)
        self.inbox, self.outbox, self.send, self.recv, self.local = inbox, outbox, send, recv, local
        self.stage, self.peak, self.scale = work
        self.count = n - 1
        self.group = 128 // r
        self.groups = 16 // self.group

    def copy(self, way, m):
        return pltpu.make_async_remote_copy(
            src_ref=self.outbox.at[way, m],
            dst_ref=self.inbox.at[way, m],
            send_sem=self.send.at[way, m],
            recv_sem=self.recv.at[way, m],
            device_id=self.to[way],
            device_id_type=MESH,
        )

    def open(self, way, m, slot):
        steps = self.inbox[way, m, pl.ds(16 * self.r, 16), :].astype(jnp.int32).astype(F32)
        self.scale[slot] = jnp.exp(steps * (1.0 / 128)) * (1.0 / 32760)

    def spread(self, i, slot):
        rows = [self.scale[slot, pl.ds(i * self.group + q, 1), :] for q in range(self.group)]
        return jnp.concatenate([jnp.broadcast_to(row, (self.r, 128)) for row in rows], axis=0)

    def taken(self, way, m, i, slot):
        data = self.inbox[way, m, pl.ds(pl.multiple_of(i * 128, 128), 128), :]
        return data.astype(jnp.int32).astype(F32) * self.spread(i, slot)

    def own(self, step, half, i):
        return self.local(step, half * 16 + i * self.group, self.group).reshape(128, 128)

    def emit(self, m):
        hops = self.n // 2 - (m + 1) // 2
        for way in (0, 1):
            half = way if m % 2 == 0 else 1 - way
            step = hops if way == 0 else self.n - hops
            if m >= 2:
                self.copy(way, m - 2).wait_recv()
                self.open(way, m - 2, 0)

            def add(i, _):
                value = self.own(step, half, i)
                if m >= 2:
                    value = value + self.taken(way, m - 2, i, 0)
                self.stage[pl.ds(pl.multiple_of(i * 128, 128), 128), :] = value
                size = jnp.abs(value)
                for q in range(self.group):
                    self.peak[pl.ds(i * self.group + q, 1), :] = jnp.max(
                        size[q * self.r:(q + 1) * self.r], axis=0, keepdims=True
                    )
                return 0

            lax.fori_loop(0, self.groups, add, 0)
            steps = jnp.ceil(jnp.log(jnp.maximum(self.peak[...], 1e-30)) * 128)
            self.scale[1] = jnp.exp(steps * (-1.0 / 128)) * 32760
            self.outbox[way, m, pl.ds(16 * self.r, 16), :] = steps.astype(jnp.int32).astype(I16)

            def code(i, _):
                rows = pl.ds(pl.multiple_of(i * 128, 128), 128)
                value = jnp.round(self.stage[rows, :] * self.spread(i, 1))
                self.outbox[way, m, rows, :] = value.astype(jnp.int32).astype(I16)
                return 0

            lax.fori_loop(0, self.groups, code, 0)
            self.copy(way, m).start()

    def finish(self, store):
        last = self.count - 1
        for half in (0, 1):
            first = last if half == 0 else last - 1
            second = last - 1 if half == 0 else last
            self.copy(0, first).wait_recv()
            self.copy(1, second).wait_recv()
            self.open(0, first, 0)
            self.open(1, second, 1)

            def body(i, _):
                value = self.own(0, half, i)
                value = value + self.taken(0, first, i, 0) + self.taken(1, second, i, 1)
                store(half * 16 + i * self.group, value.reshape(self.group, self.r, 128))
                return 0

            lax.fori_loop(0, self.groups, body, 0)

    def drain(self):
        for way in (0, 1):
            for m in range(self.count):
                self.copy(way, m).wait_send()


def reduce_part(
    g_ref, left_ref, right_ref, gm_ref, a,
    stage, peak, scale, own_a, got_a, own_b, got_b, sum_a, sum_b,
    az_in, az_out, ax_in, ax_out, bx_in, bx_out, bz_in, bz_out,
    az_s, az_r, ax_s, ax_r, bx_s, bx_r, bz_s, bz_r,
    load_a, load_b, swap_a_s, swap_a_r, swap_b_s, swap_b_r, stat_s, stat_r, load_sem,
):
    x, z, c, y = place()
    partner = device(x, z, 1 - c, y)
    zr, zl = device(x, (z + 1) % NZ, c, y), device(x, (z + NZ - 1) % NZ, c, y)
    xr, xl = device((x + 1) % NX, z, c, y), device((x + NX - 1) % NX, z, c, y)

    def slice_a(core, rel):
        start = core * 256 + ((z + rel) % NZ) * 32
        return g_ref.at[0, pl.ds(0, 32), pl.ds(pl.multiple_of(start, 32), 32)]

    def slice_b(core, rel):
        start = core * 256 + ((x + rel) % NX) * 64
        return g_ref.at[0, pl.ds(32, 32), pl.ds(pl.multiple_of(start, 64), 64)]

    def load(kind, rel):
        if kind == "a":
            return pltpu.make_async_copy(slice_a(c, rel), own_a.at[rel], load_a.at[rel])
        return pltpu.make_async_copy(slice_b(c, rel), own_b.at[rel], load_b.at[rel])

    def swap(kind, rel):
        source, target, s, r = (
            (slice_a(1 - c, rel), got_a, swap_a_s, swap_a_r)
            if kind == "a"
            else (slice_b(1 - c, rel), got_b, swap_b_s, swap_b_r)
        )
        return pltpu.make_async_remote_copy(
            src_ref=source, dst_ref=target.at[rel], send_sem=s.at[rel], recv_sem=r.at[rel],
            device_id=partner, device_id_type=MESH,
        )

    order = [("a", 4), ("b", 2), ("a", 3), ("a", 5), ("b", 1), ("b", 3),
             ("a", 2), ("a", 6), ("a", 1), ("a", 7), ("b", 0), ("a", 0)]
    for kind, rel in order[:AHEAD]:
        swap(kind, rel).start()
        load(kind, rel).start()
    ahead = list(order[AHEAD:])

    mine = (y // 2) == c

    def keep(source):
        return pltpu.make_async_copy(source.at[0, y % 2], a, load_sem)

    def give(source):
        return pltpu.make_async_remote_copy(
            src_ref=source.at[0, y % 2], dst_ref=a, send_sem=stat_s, recv_sem=stat_r,
            device_id=partner, device_id_type=MESH,
        )

    def statistic():
        @pl.when(mine & (c == 0))
        def _():
            keep(left_ref).start()
            give(right_ref).start()

        @pl.when(mine & (c == 1))
        def _():
            keep(right_ref).start()
            give(left_ref).start()

    def need(*pieces):
        for kind, rel in pieces:
            load(kind, rel).wait()
            swap(kind, rel).wait_recv()
            if ahead:
                swap(*ahead[0]).start()
                load(*ahead.pop(0)).start()

    def local_az(rel, block, count):
        blocks = pl.ds(block, count)
        return own_a[rel, blocks].astype(F32) + got_a[rel, blocks].astype(F32)

    def local_bx(rel, block, count):
        blocks = pl.ds(block, count)
        return own_b[rel, blocks].astype(F32) + got_b[rel, blocks].astype(F32)

    def local_ax(rel, block, count):
        return sum_a[pl.ds(block, count), pl.ds(pl.multiple_of(((x + rel) % NX) * 8, 8), 8)]

    def local_bz(rel, block, count):
        return sum_b[pl.ds(block, count), pl.ds(pl.multiple_of(((z + rel) % NZ) * 8, 8), 8)]

    work = (stage, peak, scale)
    az = Ring(NZ, 32, zr, zl, az_in, az_out, az_s, az_r, local_az, work)
    bx = Ring(NX, 64, xr, xl, bx_in, bx_out, bx_s, bx_r, local_bx, work)
    ax = Ring(NX, 8, xr, xl, ax_in, ax_out, ax_s, ax_r, local_ax, work)
    bz = Ring(NZ, 8, zr, zl, bz_in, bz_out, bz_s, bz_r, local_bz, work)

    need(("a", 4))
    az.emit(0)
    need(("b", 2))
    bx.emit(0)
    need(("a", 3), ("a", 5))
    az.emit(1)
    need(("b", 1), ("b", 3))
    bx.emit(1)
    az.emit(2)
    need(("a", 2), ("a", 6))
    az.emit(3)
    bx.emit(2)
    az.emit(4)
    need(("a", 1), ("a", 7))
    statistic()
    az.emit(5)
    az.emit(6)
    need(("b", 0), ("a", 0))

    def store_b(block, value):
        sum_b[pl.ds(block, 2)] = value

    def store_a(block, value):
        sum_a[pl.ds(block, 4)] = value

    def done_a(block, value):
        gm_ref[pl.ds(block, 16)] = value * (1.0 / 64)

    def done_b(block, value):
        gm_ref[pl.ds(32 + block, 16)] = value * (1.0 / 64)

    bx.finish(store_b)
    bz.emit(0)
    bz.emit(1)
    az.finish(store_a)
    ax.emit(0)
    ax.emit(1)
    bz.emit(2)
    bz.emit(3)
    ax.emit(2)
    bz.emit(4)
    ax.finish(done_a)
    bz.emit(5)
    bz.emit(6)
    bz.finish(done_b)
    def settle():
        for ring in (az, bx, ax, bz):
            ring.drain()
        for kind, rel in order:
            swap(kind, rel).wait_send()

        @pl.when(mine)
        def _():
            keep(left_ref).wait()
            give(left_ref).wait_send()

        @pl.when((y // 2) != c)
        def _():
            give(left_ref).wait_recv()

    return settle


def split(value):
    high = value.astype(BF16)
    return high, (value - high.astype(F32)).astype(BF16)


def dot(a, b, dims=((1,), (0,))):
    return lax.dot_general(a, b, (dims, ((), ())), preferred_element_type=F32)


def product(a, b, rows, dims=((1,), (0,)), columns=None):
    part = (rows, slice(None)) if columns is None else (slice(None), columns)
    ah, al = a[0][part], a[1][part]
    bh, bl = b[0][...], b[1][...]
    return dot(ah, bh, dims) + (dot(ah, bl, dims) + dot(al, bh, dims))


def diagonal(start, count):
    row = start + lax.broadcasted_iota(jnp.int32, (count, 512), 0)
    return row == lax.broadcasted_iota(jnp.int32, (count, 512), 1)


def tiles(body, count, init=0):
    size = 512 // count

    def step(i, carry):
        start = pl.multiple_of(i * size, size)
        return body(i, start, pl.ds(start, size), carry)

    return lax.fori_loop(0, count, step, init)


def total(value):
    return jnp.sum(jnp.sum(value, axis=0, keepdims=True), axis=1, keepdims=True)


def owner_part(
    settle, inv_ref, owners_ref, slots_ref, gm_ref, a, out_ref,
    outp, xb, zout, zb, hb, g, gh, gl, ah, al, a2, sh, sl, fh, fl, th, tl, qh, ql,
    roots, uh, ul, outv, wb, outw, rb, fin,
    x_s, x_r, z_s, z_r, p_s, p_r, r_s, r_r, w_s, w_r, b_s, b_r,
):
    x, z, c, y = place()
    partner = device(x, z, 1 - c, y)

    def row(dx):
        return (x + dx) % NX

    def send(source, target, sems, where, to):
        return pltpu.make_async_remote_copy(
            src_ref=source, dst_ref=target, send_sem=sems[0].at[where], recv_sem=sems[1].at[where],
            device_id=to, device_id_type=MESH,
        )

    def to_plane(dx, d):
        return device(row(dx), z, c, (y + d) % NY)

    def to_z(dz):
        return device(x, (z + dz) % NZ, c, y)

    plane = [(dx, d) for dx in range(NX) for d in range(NY)]

    def along_xy(dx, d, q):
        return send(outp.at[q, dx * NY + d], xb.at[q, x * NY + y], (x_s, x_r), q, to_plane(dx, d))

    def all_xy(q):
        others = pl.ds(0, NX * NY - 1)
        return send(outp.at[q, others], xb.at[q, others], (x_s, x_r), q, to_plane(0, 1))

    def along_z(dz):
        return send(zout.at[dz - 1], zb.at[c, z], (z_s, z_r), dz - 1, to_z(dz))

    def across(dz):
        part = zb.at[c, (z + NZ - dz) % NZ]
        return send(part, part, (p_s, p_r), dz, partner)

    def forward_xy(q):
        for dx, d in plane:
            for e, dz in enumerate(FORWARD[q]):
                there = (row(dx) * NZ + (z + dz) % NZ) * 4 + (y + d) % NY
                outp[q, dx * NY + d, e] = gm_ref[inv_ref[0, there]]
            if dx or d:
                along_xy(dx, d, q).start()
            else:
                xb[q, x * NY + y] = outp[q, 0]

    def forward_z(q):
        all_xy(q).wait_recv()
        for e, dz in enumerate(FORWARD[q]):
            value = xb[q, :, e].reshape(128, 128)
            peak = jnp.max(jnp.abs(value), axis=0, keepdims=True)
            steps = jnp.ceil(jnp.log(jnp.maximum(peak, 1e-30)) * 128)
            value = jnp.round(value * (jnp.exp(steps * (-1.0 / 128)) * 32760))
            value = jnp.concatenate([value, jnp.broadcast_to(steps, (16, 128))], axis=0)
            value = value.astype(jnp.int32).astype(I16)
            if dz:
                zout[dz - 1] = value
                along_z(dz).start()
            else:
                zb[c, z] = value
                across(0).start()

    forward_xy(0)
    for q in range(1, len(FORWARD)):
        forward_xy(q)
        forward_z(q - 1)
    forward_z(len(FORWARD) - 1)

    def decode(core, zz):
        steps = zb[core, zz, pl.ds(128, 16), :].astype(jnp.int32).astype(F32)[:1]
        scale = jnp.exp(steps * (1.0 / 128)) * (1.0 / 32760)
        value = zb[core, zz, pl.ds(0, 128), :].astype(jnp.int32).astype(F32) * scale
        hb[core, zz] = value.reshape(16, 8, 128)

    decode(c, z)
    settle()
    for dz in (1, 7, 2, 6, 3, 5, 4):
        along_z(dz).wait_recv()
        across(dz).start()
        decode(c, (z + NZ - dz) % NZ)
    for dz in (0, 1, 7, 2, 6, 3, 5, 4):
        across(dz).wait_recv()
        decode(1 - c, (z + NZ - dz) % NZ)

    early = inv_ref[0, (x * NZ + z) * 4 + y] < 32

    def assemble(p, _):
        piece = jnp.where(early, p, (p % NZ) * NX + p // NZ) * 4
        for core in range(2):
            start = pl.multiple_of(core * 256 + p * 8, 8)
            for yy in range(NY):
                g[pl.ds(start, 8), yy * 128:yy * 128 + 128] = hb[core, piece // 16, piece % 16 + yy]
        return 0

    lax.fori_loop(0, 32, assemble, 0)

    def split_g(i, start, rows, squares):
        value = g[rows, :]
        gh[rows, :], gl[rows, :] = split(value)
        return squares + total(value * value)

    zero = jnp.zeros((1, 1), F32)
    grad_squares = tiles(split_g, 8, zero)

    pair_g = (gh, gl)

    def rows_of(i):
        return pl.ds(i * 256, 256)

    @pl.when(c == 0)
    def _():
        for i in range(2):
            a[rows_of(i), :] = 0.95 * a[rows_of(i), :] + product(pair_g, pair_g, rows_of(i), ((1,), (1,)))

    @pl.when(c == 1)
    def _():
        for i in range(2):
            a[rows_of(i), :] = 0.95 * a[rows_of(i), :] + product(
                pair_g, pair_g, None, ((0,), (0,)), columns=rows_of(i)
            )

    def trace_of(i, start, rows, trace):
        return trace + total(jnp.where(diagonal(start, 64), a[rows, :], 0.0))

    size = tiles(trace_of, 8, zero) * (1.0 / 512)
    scale = 1.0 / size

    def split_a(i, start, rows, carry):
        value = a[rows, :] * scale
        a[rows, :] = value
        ah[rows, :], al[rows, :] = split(value)
        return carry

    tiles(split_a, 8)
    pair_a = (ah, al)

    def square(i, start, rows, carry):
        a2[rows, :] = product(pair_a, pair_a, rows)
        return carry

    tiles(square, 1)

    def unit(image):
        return image / jnp.sqrt(total(image * image))

    vector = jnp.full((1, 512), 512 ** (-0.5), F32)
    vector = unit(jnp.sum(a2[...] * vector, axis=1, keepdims=True))
    vector = unit(jnp.sum(a2[...] * vector, axis=0, keepdims=True))
    vector = unit(jnp.sum(a2[...] * vector, axis=1, keepdims=True))
    image = jnp.sum(a[...] * vector, axis=0, keepdims=True)
    flat = jnp.sum(jnp.where(diagonal(0, 512), vector, 0.0), axis=0, keepdims=True)
    largest = total(flat * image)
    factor = 2.5 / largest
    fourth = jnp.sqrt(jnp.sqrt(factor * scale))

    def first_terms(i, start, rows, carry):
        eye = jnp.where(diagonal(start, 64), 1.0, 0.0)
        value = a[rows, :] * factor
        qh[rows, :], ql[rows, :] = split(1.25 * eye - 0.25 * value)
        squared = (25.0 / 16) * eye - (10.0 / 16) * value + (factor * factor * (1.0 / 16)) * a2[rows, :]
        sh[rows, :], sl[rows, :] = split(squared)
        return carry

    tiles(first_terms, 8)

    def power_four(i, start, rows, carry):
        fh[rows, :], fl[rows, :] = split(product((sh, sl), (sh, sl), rows))
        return carry

    tiles(power_four, 1)

    def second_term(i, start, rows, carry):
        value = product((fh, fl), pair_a, rows) * (0.25 * factor)
        th[rows, :], tl[rows, :] = split(jnp.where(diagonal(start, 512), 1.25, 0.0) - value)
        return carry

    tiles(second_term, 1)

    def send_root(i):
        part = roots.at[c, :, pl.ds(i * 256, 256)]
        return pltpu.make_async_remote_copy(
            src_ref=part, dst_ref=part, send_sem=r_s.at[i], recv_sem=r_r.at[i],
            device_id=partner, device_id_type=MESH,
        )

    for i in range(2):
        rows = rows_of(i)
        high, low = split(product((qh, ql), (th, tl), rows) * fourth)
        roots[c, 0, rows, :] = high
        roots[c, 1, rows, :] = low
        send_root(i).start()

    pair_l = (roots.at[0, 0], roots.at[0, 1])
    pair_r = (roots.at[1, 0], roots.at[1, 1])
    pair_u = (uh, ul)

    def middle(one, two):
        def body(i, start, rows, carry):
            uh[rows, :], ul[rows, :] = split(product(one, two, rows))
            return carry

        tiles(body, 1)

    @pl.when(c == 0)
    def _():
        middle(pair_l, pair_g)

    @pl.when(c == 1)
    def _():
        middle(pair_g, pair_r)

    for i in range(2):
        send_root(i).wait_recv()

    def outer(one, two):
        def body(i, start, rows, carry):
            a2[rows, :] = product(one, two, rows)
            return carry

        tiles(body, 1)

    @pl.when(c == 0)
    def _():
        outer(pair_u, pair_r)

    @pl.when(c == 1)
    def _():
        outer(pair_l, pair_u)

    def squares_of(i, start, rows, carry):
        value = a2[rows, :]
        return carry + total(value * value)

    ratio = jnp.sqrt((grad_squares + 1e-06) / (tiles(squares_of, 8, zero) + 1e-06))

    def back_xy(dx, d, q):
        return send(outv.at[q, dx * NY + d], wb.at[q, x * NY + y], (w_s, w_r), q, to_plane(dx, d))

    def all_back(q):
        others = pl.ds(0, NX * NY - 1)
        return send(outv.at[q, others], wb.at[q, others], (w_s, w_r), q, to_plane(0, 1))

    def back_z(dz):
        return send(outw.at[dz], rb.at[z], (b_s, b_r), dz - 1, to_z(dz))

    def return_xy(q):
        for dx, d in plane:
            column = pl.ds(pl.multiple_of(((y + d) % NY) * 128, 128), 128)
            two = [
                a2[pl.ds(pl.multiple_of((row(dx) * NZ + (z + dz) % NZ) * 16 + c * 8, 8), 8), column]
                for dz in BACK[q]
            ]
            outv[q, dx * NY + d] = (jnp.concatenate(two, axis=0) * ratio).astype(BF16)
            if dx or d:
                back_xy(dx, d, q).start()
            else:
                wb[q, x * NY + y] = outv[q, 0]

    def return_z(q):
        all_back(q).wait_recv()
        value = wb[q].astype(F32).reshape(16, len(BACK[0]), 8, 128)
        for e, dz in enumerate(BACK[q]):
            part = value[:, e].reshape(128, 128).astype(BF16)
            if dz:
                outw[dz] = part
                back_z(dz).start()
            else:
                rb[z] = part

    return_xy(0)
    for q in range(1, len(BACK)):
        return_xy(q)
        return_z(q - 1)
    return_z(len(BACK) - 1)
    for q in range(len(FORWARD)):
        all_xy(q).wait_send()
    for dz in range(NZ):
        if dz:
            along_z(dz).wait_send()
        across(dz).wait_send()
    for i in range(2):
        send_root(i).wait_send()
    for dz in (1, 7, 2, 6, 3, 5, 4):
        back_z(dz).wait_recv()

    def unpack(i, _):
        fin[pl.ds(i * 16, 16)] = rb[i].astype(F32).reshape(16, 8, 128)
        return 0

    lax.fori_loop(0, NZ, unpack, 0)

    def pick(k, _):
        owner, slot = owners_ref[k], slots_ref[k]
        chip = owner // 2
        out_ref[k] = fin[(chip % NZ) * 16 + (chip // NZ) * 4 + (owner % 2) * 2 + slot].astype(BF16)
        return 0

    lax.fori_loop(0, 64, pick, 0)

    for q in range(len(BACK)):
        all_back(q).wait_send()
    for dz in range(1, NZ):
        back_z(dz).wait_send()


OWNER_SCRATCH = 39


def kernel(owners_ref, slots_ref, g_ref, left_ref, right_ref, out_ref, gm, a, table, inv, table_sem, *scratch):
    x, z, c, y = place()
    others = [device(x, z, 1 - c, y)]
    others += [
        device((x + dx) % NX, z, c, (y + d) % NY) for dx in range(NX) for d in range(NY) if dx or d
    ]
    others += [device(x, (z + d) % NZ, c, y) for d in range(1, NZ)]
    barrier = pltpu.get_barrier_semaphore()
    for other in others:
        pl.semaphore_signal(barrier, inc=1, device_id=other, device_id_type=MESH)

    lane = lax.broadcasted_iota(jnp.int32, (8, 128), 1)

    def note(k, found):
        return jnp.where(lane == owners_ref[k] * CAP + slots_ref[k], k, found)

    table[...] = lax.fori_loop(0, 64, note, jnp.zeros((8, 128), jnp.int32))
    lookup = pltpu.make_async_copy(table, inv, table_sem)
    lookup.start()
    lookup.wait()
    pl.semaphore_wait(barrier, len(others))
    ring = len(scratch) - OWNER_SCRATCH
    settle = reduce_part(g_ref, left_ref, right_ref, gm, a, *scratch[:ring])
    owner_part(settle, inv, owners_ref, slots_ref, gm, a, out_ref, *scratch[ring:])


def step(owners, slots, grads, left_stats, right_stats):
    vm = pltpu.VMEM
    dma = pltpu.SemaphoreType.DMA
    hbm = pl.BlockSpec(memory_space=pltpu.HBM)
    smem = pl.BlockSpec(memory_space=pltpu.SMEM)
    full, half = vm((512, 512), F32), vm((512, 512), BF16)

    def boxes(count, r):
        return [vm((2, count, 16 * r + 16, 128), I16)] * 2

    ring = [
        vm((1024, 128), F32), vm((16, 128), F32), vm((2, 16, 128), F32),
        vm((8, 32, 32, 128), BF16), vm((8, 32, 32, 128), BF16),
        vm((4, 32, 64, 128), BF16), vm((4, 32, 64, 128), BF16),
        vm((32, 32, 128), F32), vm((32, 64, 128), F32),
        *boxes(7, 32), *boxes(3, 8), *boxes(3, 64), *boxes(7, 8),
        dma((2, 7)), dma((2, 7)), dma((2, 3)), dma((2, 3)),
        dma((2, 3)), dma((2, 3)), dma((2, 7)), dma((2, 7)),
        dma((8,)), dma((4,)), dma((8,)), dma((8,)), dma((4,)), dma((4,)), dma, dma, dma,
    ]
    f_parts, b_parts = len(FORWARD), len(BACK)
    part = vm((b_parts, 16, 64 // b_parts, 128), BF16)
    piece = vm((f_parts, 16, 8 // f_parts, 8, 128), F32)
    owner = [
        piece, piece,
        vm((7, 144, 128), I16), vm((2, 8, 144, 128), I16), vm((2, 8, 16, 8, 128), F32),
        full, half, half, half, half, full,
        half, half, half, half, half, half, half, half,
        vm((2, 2, 512, 512), BF16), half, half,
        part, part, vm((8, 128, 128), BF16), vm((8, 128, 128), BF16), vm((128, 8, 128), F32),
        dma((f_parts,)), dma((f_parts,)), dma((7,)), dma((7,)), dma((8,)), dma((8,)),
        dma((2,)), dma((2,)), dma((b_parts,)), dma((b_parts,)), dma((7,)), dma((7,)),
    ]
    assert len(owner) == OWNER_SCRATCH
    return pl.pallas_call(
        kernel,
        out_shape=jax.ShapeDtypeStruct((64, 8, 128), BF16),
        in_specs=[smem, smem, hbm, hbm, hbm],
        out_specs=pl.BlockSpec(memory_space=pltpu.VMEM),
        scratch_shapes=[
            vm((64, 8, 128), F32), full, vm((8, 128), jnp.int32), pltpu.SMEM((8, 128), jnp.int32), dma, *ring, *owner
        ],
        compiler_params=pltpu.CompilerParams(
            collective_id=0, has_side_effects=True, vmem_limit_bytes=56 * 1024 * 1024
        ),
        name="shampoo_step",
    )(owners, slots, grads, left_stats, right_stats)


def shards(grads, left_stats, right_stats, owners, slots):
    return step(owners, slots, grads, left_stats, right_stats)


def solution(mesh):
    in_specs = (
        P("dp", None, None, "mp"),
        P("dp", None, None, None),
        P("dp", None, None, None),
        P(),
        P(),
    )
    out_specs = P(None, "dp", "mp")
    return jax.shard_map(shards, mesh=mesh, in_specs=in_specs, out_specs=out_specs, check_vma=False)
```

```python
import jax
import jax.numpy as jnp
from jax import lax
from jax.experimental import pallas as pl
from jax.experimental.pallas import tpu as pltpu
from jax.sharding import PartitionSpec as P

CAP = 2
NX, NZ, NY = 4, 8, 4
AHEAD = 5
FORWARD = ((4, 5, 3, 6), (2, 7, 1, 0))
BACK = ((4, 5, 3, 6), (2, 7, 1, 0))
MESH = pl.DeviceIdType.MESH
F32 = jnp.float32
BF16 = jnp.bfloat16
I16 = jnp.int16


def place():
    dp = lax.axis_index("dp")
    chip = dp // 2
    return chip // NZ, chip % NZ, dp % 2, lax.axis_index("mp")


def device(x, z, c, y):
    return ((x * NZ + z) * 2 + c, y)


class Ring:
    def __init__(self, n, r, right, left, inbox, outbox, send, recv, local, work):
        self.n, self.r, self.to = n, r, (right, left)
        self.inbox, self.outbox, self.send, self.recv, self.local = inbox, outbox, send, recv, local
        self.stage, self.peak, self.scale = work
        self.count = n - 1
        self.group = 128 // r
        self.groups = 16 // self.group

    def copy(self, way, m):
        return pltpu.make_async_remote_copy(
            src_ref=self.outbox.at[way, m],
            dst_ref=self.inbox.at[way, m],
            send_sem=self.send.at[way, m],
            recv_sem=self.recv.at[way, m],
            device_id=self.to[way],
            device_id_type=MESH,
        )

    def open(self, way, m, slot):
        steps = self.inbox[way, m, pl.ds(16 * self.r, 16), :].astype(jnp.int32).astype(F32)
        self.scale[slot] = jnp.exp(steps * (1.0 / 128)) * (1.0 / 32760)

    def spread(self, i, slot):
        rows = [self.scale[slot, pl.ds(i * self.group + q, 1), :] for q in range(self.group)]
        return jnp.concatenate([jnp.broadcast_to(row, (self.r, 128)) for row in rows], axis=0)

    def taken(self, way, m, i, slot):
        data = self.inbox[way, m, pl.ds(pl.multiple_of(i * 128, 128), 128), :]
        return data.astype(jnp.int32).astype(F32) * self.spread(i, slot)

    def own(self, step, half, i):
        return self.local(step, half * 16 + i * self.group, self.group).reshape(128, 128)

    def emit(self, m):
        hops = self.n // 2 - (m + 1) // 2
        for way in (0, 1):
            half = way if m % 2 == 0 else 1 - way
            step = hops if way == 0 else self.n - hops
            if m >= 2:
                self.copy(way, m - 2).wait_recv()
                self.open(way, m - 2, 0)

            def add(i, _):
                value = self.own(step, half, i)
                if m >= 2:
                    value = value + self.taken(way, m - 2, i, 0)
                self.stage[pl.ds(pl.multiple_of(i * 128, 128), 128), :] = value
                size = jnp.abs(value)
                for q in range(self.group):
                    self.peak[pl.ds(i * self.group + q, 1), :] = jnp.max(
                        size[q * self.r:(q + 1) * self.r], axis=0, keepdims=True
                    )
                return 0

            lax.fori_loop(0, self.groups, add, 0)
            steps = jnp.ceil(jnp.log(jnp.maximum(self.peak[...], 1e-30)) * 128)
            self.scale[1] = jnp.exp(steps * (-1.0 / 128)) * 32760
            self.outbox[way, m, pl.ds(16 * self.r, 16), :] = steps.astype(jnp.int32).astype(I16)

            def code(i, _):
                rows = pl.ds(pl.multiple_of(i * 128, 128), 128)
                value = jnp.round(self.stage[rows, :] * self.spread(i, 1))
                self.outbox[way, m, rows, :] = value.astype(jnp.int32).astype(I16)
                return 0

            lax.fori_loop(0, self.groups, code, 0)
            self.copy(way, m).start()

    def finish(self, store):
        last = self.count - 1
        for half in (0, 1):
            first = last if half == 0 else last - 1
            second = last - 1 if half == 0 else last
            self.copy(0, first).wait_recv()
            self.copy(1, second).wait_recv()
            self.open(0, first, 0)
            self.open(1, second, 1)

            def body(i, _):
                value = self.own(0, half, i)
                value = value + self.taken(0, first, i, 0) + self.taken(1, second, i, 1)
                store(half * 16 + i * self.group, value.reshape(self.group, self.r, 128))
                return 0

            lax.fori_loop(0, self.groups, body, 0)

    def drain(self):
        for way in (0, 1):
            for m in range(self.count):
                self.copy(way, m).wait_send()


def reduce_part(
    g_ref, left_ref, right_ref, gm_ref, a,
    stage, peak, scale, own_a, got_a, own_b, got_b, sum_a, sum_b,
    az_in, az_out, ax_in, ax_out, bx_in, bx_out, bz_in, bz_out,
    az_s, az_r, ax_s, ax_r, bx_s, bx_r, bz_s, bz_r,
    load_a, load_b, swap_a_s, swap_a_r, swap_b_s, swap_b_r, stat_s, stat_r, load_sem,
):
    x, z, c, y = place()
    partner = device(x, z, 1 - c, y)
    zr, zl = device(x, (z + 1) % NZ, c, y), device(x, (z + NZ - 1) % NZ, c, y)
    xr, xl = device((x + 1) % NX, z, c, y), device((x + NX - 1) % NX, z, c, y)

    def slice_a(core, rel):
        start = core * 256 + ((z + rel) % NZ) * 32
        return g_ref.at[0, pl.ds(0, 32), pl.ds(pl.multiple_of(start, 32), 32)]

    def slice_b(core, rel):
        start = core * 256 + ((x + rel) % NX) * 64
        return g_ref.at[0, pl.ds(32, 32), pl.ds(pl.multiple_of(start, 64), 64)]

    def load(kind, rel):
        if kind == "a":
            return pltpu.make_async_copy(slice_a(c, rel), own_a.at[rel], load_a.at[rel])
        return pltpu.make_async_copy(slice_b(c, rel), own_b.at[rel], load_b.at[rel])

    def swap(kind, rel):
        source, target, s, r = (
            (slice_a(1 - c, rel), got_a, swap_a_s, swap_a_r)
            if kind == "a"
            else (slice_b(1 - c, rel), got_b, swap_b_s, swap_b_r)
        )
        return pltpu.make_async_remote_copy(
            src_ref=source, dst_ref=target.at[rel], send_sem=s.at[rel], recv_sem=r.at[rel],
            device_id=partner, device_id_type=MESH,
        )

    order = [("a", 4), ("b", 2), ("a", 3), ("a", 5), ("b", 1), ("b", 3),
             ("a", 2), ("a", 6), ("a", 1), ("a", 7), ("b", 0), ("a", 0)]
    for kind, rel in order[:AHEAD]:
        swap(kind, rel).start()
        load(kind, rel).start()
    ahead = list(order[AHEAD:])

    mine = (y // 2) == c

    def keep(source):
        return pltpu.make_async_copy(source.at[0, y % 2], a, load_sem)

    def give(source):
        return pltpu.make_async_remote_copy(
            src_ref=source.at[0, y % 2], dst_ref=a, send_sem=stat_s, recv_sem=stat_r,
            device_id=partner, device_id_type=MESH,
        )

    def statistic():
        @pl.when(mine & (c == 0))
        def _():
            keep(left_ref).start()
            give(right_ref).start()

        @pl.when(mine & (c == 1))
        def _():
            keep(right_ref).start()
            give(left_ref).start()

    def need(*pieces):
        for kind, rel in pieces:
            load(kind, rel).wait()
            swap(kind, rel).wait_recv()
            if ahead:
                swap(*ahead[0]).start()
                load(*ahead.pop(0)).start()

    def local_az(rel, block, count):
        blocks = pl.ds(block, count)
        return own_a[rel, blocks].astype(F32) + got_a[rel, blocks].astype(F32)

    def local_bx(rel, block, count):
        blocks = pl.ds(block, count)
        return own_b[rel, blocks].astype(F32) + got_b[rel, blocks].astype(F32)

    def local_ax(rel, block, count):
        return sum_a[pl.ds(block, count), pl.ds(pl.multiple_of(((x + rel) % NX) * 8, 8), 8)]

    def local_bz(rel, block, count):
        return sum_b[pl.ds(block, count), pl.ds(pl.multiple_of(((z + rel) % NZ) * 8, 8), 8)]

    work = (stage, peak, scale)
    az = Ring(NZ, 32, zr, zl, az_in, az_out, az_s, az_r, local_az, work)
    bx = Ring(NX, 64, xr, xl, bx_in, bx_out, bx_s, bx_r, local_bx, work)
    ax = Ring(NX, 8, xr, xl, ax_in, ax_out, ax_s, ax_r, local_ax, work)
    bz = Ring(NZ, 8, zr, zl, bz_in, bz_out, bz_s, bz_r, local_bz, work)

    need(("a", 4))
    az.emit(0)
    need(("b", 2))
    bx.emit(0)
    need(("a", 3), ("a", 5))
    az.emit(1)
    need(("b", 1), ("b", 3))
    bx.emit(1)
    az.emit(2)
    need(("a", 2), ("a", 6))
    az.emit(3)
    bx.emit(2)
    az.emit(4)
    need(("a", 1), ("a", 7))
    statistic()
    az.emit(5)
    az.emit(6)
    need(("b", 0), ("a", 0))

    def store_b(block, value):
        sum_b[pl.ds(block, 2)] = value

    def store_a(block, value):
        sum_a[pl.ds(block, 4)] = value

    def done_a(block, value):
        gm_ref[pl.ds(block, 16)] = value * (1.0 / 64)

    def done_b(block, value):
        gm_ref[pl.ds(32 + block, 16)] = value * (1.0 / 64)

    bx.finish(store_b)
    bz.emit(0)
    bz.emit(1)
    az.finish(store_a)
    ax.emit(0)
    ax.emit(1)
    bz.emit(2)
    bz.emit(3)
    ax.emit(2)
    bz.emit(4)
    ax.finish(done_a)
    bz.emit(5)
    bz.emit(6)
    bz.finish(done_b)
    def settle():
        for ring in (az, bx, ax, bz):
            ring.drain()
        for kind, rel in order:
            swap(kind, rel).wait_send()

        @pl.when(mine)
        def _():
            keep(left_ref).wait()
            give(left_ref).wait_send()

        @pl.when((y // 2) != c)
        def _():
            give(left_ref).wait_recv()

    return settle


def split(value):
    high = value.astype(BF16)
    return high, (value - high.astype(F32)).astype(BF16)


def dot(a, b, dims=((1,), (0,))):
    return lax.dot_general(a, b, (dims, ((), ())), preferred_element_type=F32)


def product(a, b, rows, dims=((1,), (0,)), columns=None):
    part = (rows, slice(None)) if columns is None else (slice(None), columns)
    ah, al = a[0][part], a[1][part]
    bh, bl = b[0][...], b[1][...]
    return dot(ah, bh, dims) + (dot(ah, bl, dims) + dot(al, bh, dims))


def diagonal(start, count):
    row = start + lax.broadcasted_iota(jnp.int32, (count, 512), 0)
    return row == lax.broadcasted_iota(jnp.int32, (count, 512), 1)


def tiles(body, count, init=0):
    size = 512 // count

    def step(i, carry):
        start = pl.multiple_of(i * size, size)
        return body(i, start, pl.ds(start, size), carry)

    return lax.fori_loop(0, count, step, init)


def total(value):
    return jnp.sum(jnp.sum(value, axis=0, keepdims=True), axis=1, keepdims=True)


def owner_part(
    settle, inv_ref, spot_ref, gm_ref, a, out_ref,
    outp, xb, zout, zb, hb, g, gh, gl, ah, al, a2, sh, sl, fh, fl, th, tl, qh, ql,
    roots, uh, ul, outv, wb, outw, rb, fin,
    x_s, x_r, z_s, z_r, p_s, p_r, r_s, r_r, w_s, w_r, b_s, b_r,
):
    x, z, c, y = place()
    partner = device(x, z, 1 - c, y)

    def row(dx):
        return (x + dx) % NX

    def send(source, target, sems, where, to):
        return pltpu.make_async_remote_copy(
            src_ref=source, dst_ref=target, send_sem=sems[0].at[where], recv_sem=sems[1].at[where],
            device_id=to, device_id_type=MESH,
        )

    def to_plane(dx, d):
        return device(row(dx), z, c, (y + d) % NY)

    def to_z(dz):
        return device(x, (z + dz) % NZ, c, y)

    plane = sorted(
        [(dx, d) for dx in range(NX) for d in range(NY)],
        key=lambda p: -(min(p[0], NX - p[0]) + min(p[1], NY - p[1])),
    )

    def along_xy(dx, d, q):
        return send(outp.at[q, dx * NY + d], xb.at[q, x * NY + y], (x_s, x_r), q, to_plane(dx, d))

    def all_xy(q):
        others = pl.ds(0, NX * NY - 1)
        return send(outp.at[q, others], xb.at[q, others], (x_s, x_r), q, to_plane(0, 1))

    def along_z(dz):
        return send(zout.at[dz - 1], zb.at[c, z], (z_s, z_r), dz - 1, to_z(dz))

    def across(dz):
        part = zb.at[c, (z + NZ - dz) % NZ]
        return send(part, part, (p_s, p_r), dz, partner)

    def forward_xy(q):
        for dx, d in plane:
            for e, dz in enumerate(FORWARD[q]):
                there = (row(dx) * NZ + (z + dz) % NZ) * 4 + (y + d) % NY
                outp[q, dx * NY + d, e] = gm_ref[inv_ref[0, there]]
            if dx or d:
                along_xy(dx, d, q).start()
            else:
                xb[q, x * NY + y] = outp[q, 0]

    def forward_z(q):
        all_xy(q).wait_recv()
        for e, dz in enumerate(FORWARD[q]):
            value = xb[q, :, e].reshape(128, 128)
            peak = jnp.max(jnp.abs(value), axis=0, keepdims=True)
            steps = jnp.ceil(jnp.log(jnp.maximum(peak, 1e-30)) * 128)
            value = jnp.round(value * (jnp.exp(steps * (-1.0 / 128)) * 32760))
            value = jnp.concatenate([value, jnp.broadcast_to(steps, (16, 128))], axis=0)
            value = value.astype(jnp.int32).astype(I16)
            if dz:
                zout[dz - 1] = value
                along_z(dz).start()
            else:
                zb[c, z] = value
                across(0).start()

    forward_xy(0)
    for q in range(1, len(FORWARD)):
        forward_xy(q)
        forward_z(q - 1)
    forward_z(len(FORWARD) - 1)

    def decode(core, zz):
        steps = zb[core, zz, pl.ds(128, 16), :].astype(jnp.int32).astype(F32)[:1]
        scale = jnp.exp(steps * (1.0 / 128)) * (1.0 / 32760)
        value = zb[core, zz, pl.ds(0, 128), :].astype(jnp.int32).astype(F32) * scale
        hb[core, zz] = value.reshape(16, 8, 128)

    decode(c, z)
    settle()
    for dz in (1, 7, 2, 6, 3, 5, 4):
        along_z(dz).wait_recv()
        across(dz).start()
        decode(c, (z + NZ - dz) % NZ)
    for dz in (0, 1, 7, 2, 6, 3, 5, 4):
        across(dz).wait_recv()
        decode(1 - c, (z + NZ - dz) % NZ)

    early = inv_ref[0, (x * NZ + z) * 4 + y] < 32

    def assemble(p, _):
        piece = jnp.where(early, p, (p % NZ) * NX + p // NZ) * 4
        for core in range(2):
            start = pl.multiple_of(core * 256 + p * 8, 8)
            for yy in range(NY):
                g[pl.ds(start, 8), yy * 128:yy * 128 + 128] = hb[core, piece // 16, piece % 16 + yy]
        return 0

    lax.fori_loop(0, 32, assemble, 0)

    def split_g(i, start, rows, squares):
        value = g[rows, :]
        gh[rows, :], gl[rows, :] = split(value)
        return squares + total(value * value)

    zero = jnp.zeros((1, 1), F32)
    grad_squares = tiles(split_g, 8, zero)

    pair_g = (gh, gl)

    def rows_of(i):
        return pl.ds(i * 256, 256)

    @pl.when(c == 0)
    def _():
        for i in range(2):
            a[rows_of(i), :] = 0.95 * a[rows_of(i), :] + product(pair_g, pair_g, rows_of(i), ((1,), (1,)))

    @pl.when(c == 1)
    def _():
        for i in range(2):
            a[rows_of(i), :] = 0.95 * a[rows_of(i), :] + product(
                pair_g, pair_g, None, ((0,), (0,)), columns=rows_of(i)
            )

    corner = diagonal(0, 128)[:, :128]
    size = zero
    for i in range(4):
        part = slice(i * 128, i * 128 + 128)
        size = size + total(jnp.where(corner, a[part, part], 0.0))
    size = size * (1.0 / 512)
    scale = 1.0 / size

    def split_a(i, start, rows, carry):
        value = a[rows, :] * scale
        a[rows, :] = value
        ah[rows, :], al[rows, :] = split(value)
        return carry

    tiles(split_a, 8)
    pair_a = (ah, al)

    def square(i, start, rows, carry):
        a2[rows, :] = product(pair_a, pair_a, rows)
        return carry

    tiles(square, 1)

    def unit(image):
        return image / jnp.sqrt(total(image * image))

    vector = jnp.full((1, 512), 512 ** (-0.5), F32)
    vector = unit(jnp.sum(a2[...] * vector, axis=1, keepdims=True))
    vector = unit(jnp.sum(a2[...] * vector, axis=0, keepdims=True))
    vector = unit(jnp.sum(a2[...] * vector, axis=1, keepdims=True))
    image = jnp.sum(a[...] * vector, axis=0, keepdims=True)
    flat = jnp.concatenate(
        [
            jnp.sum(jnp.where(corner, vector[i * 128:i * 128 + 128], 0.0), axis=0, keepdims=True)
            for i in range(4)
        ],
        axis=1,
    )
    largest = total(flat * image)
    factor = 2.5 / largest
    fourth = jnp.sqrt(jnp.sqrt(factor * scale))

    def first_terms(i, start, rows, carry):
        eye = jnp.where(diagonal(start, 64), 1.0, 0.0)
        value = a[rows, :] * factor
        qh[rows, :], ql[rows, :] = split(1.25 * eye - 0.25 * value)
        squared = (25.0 / 16) * eye - (10.0 / 16) * value + (factor * factor * (1.0 / 16)) * a2[rows, :]
        sh[rows, :], sl[rows, :] = split(squared)
        return carry

    tiles(first_terms, 8)

    def power_four(i, start, rows, carry):
        fh[rows, :], fl[rows, :] = split(product((sh, sl), (sh, sl), rows))
        return carry

    tiles(power_four, 1)

    def second_term(i, start, rows, carry):
        value = product((fh, fl), pair_a, rows) * (0.25 * factor)
        th[rows, :], tl[rows, :] = split(jnp.where(diagonal(start, 512), 1.25, 0.0) - value)
        return carry

    tiles(second_term, 1)

    def send_root(i):
        part = roots.at[c, :, pl.ds(i * 256, 256)]
        return pltpu.make_async_remote_copy(
            src_ref=part, dst_ref=part, send_sem=r_s.at[i], recv_sem=r_r.at[i],
            device_id=partner, device_id_type=MESH,
        )

    for i in range(2):
        rows = rows_of(i)
        high, low = split(product((qh, ql), (th, tl), rows) * fourth)
        roots[c, 0, rows, :] = high
        roots[c, 1, rows, :] = low
        send_root(i).start()

    pair_l = (roots.at[0, 0], roots.at[0, 1])
    pair_r = (roots.at[1, 0], roots.at[1, 1])
    pair_u = (uh, ul)

    def middle(one, two):
        def body(i, start, rows, carry):
            uh[rows, :], ul[rows, :] = split(product(one, two, rows))
            return carry

        tiles(body, 1)

    @pl.when(c == 0)
    def _():
        middle(pair_l, pair_g)

    @pl.when(c == 1)
    def _():
        middle(pair_g, pair_r)

    for i in range(2):
        send_root(i).wait_recv()

    def outer(one, two):
        def body(i, start, rows, carry):
            a2[rows, :] = product(one, two, rows)
            return carry

        tiles(body, 1)

    @pl.when(c == 0)
    def _():
        outer(pair_u, pair_r)

    @pl.when(c == 1)
    def _():
        outer(pair_l, pair_u)

    def squares_of(i, start, rows, carry):
        value = a2[rows, :]
        return carry + total(value * value)

    ratio = jnp.sqrt((grad_squares + 1e-06) / (tiles(squares_of, 8, zero) + 1e-06))

    def back_xy(dx, d, q):
        return send(outv.at[q, dx * NY + d], wb.at[q, x * NY + y], (w_s, w_r), q, to_plane(dx, d))

    def all_back(q):
        others = pl.ds(0, NX * NY - 1)
        return send(outv.at[q, others], wb.at[q, others], (w_s, w_r), q, to_plane(0, 1))

    def back_z(dz):
        return send(outw.at[dz], rb.at[z], (b_s, b_r), dz - 1, to_z(dz))

    def return_xy(q):
        for dx, d in plane:
            column = pl.ds(pl.multiple_of(((y + d) % NY) * 128, 128), 128)
            two = [
                a2[pl.ds(pl.multiple_of((row(dx) * NZ + (z + dz) % NZ) * 16 + c * 8, 8), 8), column]
                for dz in BACK[q]
            ]
            outv[q, dx * NY + d] = (jnp.concatenate(two, axis=0) * ratio).astype(BF16)
            if dx or d:
                back_xy(dx, d, q).start()
            else:
                wb[q, x * NY + y] = outv[q, 0]

    def return_z(q):
        all_back(q).wait_recv()
        value = wb[q].astype(F32).reshape(16, len(BACK[0]), 8, 128)
        for e, dz in enumerate(BACK[q]):
            part = value[:, e].reshape(128, 128).astype(BF16)
            if dz:
                outw[dz] = part
                back_z(dz).start()
            else:
                rb[z] = part

    return_xy(0)
    for q in range(1, len(BACK)):
        return_xy(q)
        return_z(q - 1)
    return_z(len(BACK) - 1)
    for q in range(len(FORWARD)):
        all_xy(q).wait_send()
    for dz in range(NZ):
        if dz:
            along_z(dz).wait_send()
        across(dz).wait_send()
    for i in range(2):
        send_root(i).wait_send()
    def unpack(zz):
        fin[pl.ds(zz * 16, 16)] = rb[zz].astype(F32).reshape(16, 8, 128)

    unpack(z)
    for dz in (1, 7, 2, 6, 3, 5, 4):
        back_z(dz).wait_recv()
        unpack((z + NZ - dz) % NZ)

    def pick(i, _):
        for k in range(8):
            out_ref[i * 8 + k] = fin[spot_ref[i * 8 + k]].astype(BF16)
        return 0

    lax.fori_loop(0, 8, pick, 0)

    for q in range(len(BACK)):
        all_back(q).wait_send()
    for dz in range(1, NZ):
        back_z(dz).wait_send()


OWNER_SCRATCH = 39


def kernel(owners_ref, slots_ref, g_ref, left_ref, right_ref, out_ref, gm, a, table, inv, spot, table_sem, *scratch):
    x, z, c, y = place()
    others = [device(x, z, 1 - c, y)]
    others += [
        device((x + dx) % NX, z, c, (y + d) % NY) for dx in range(NX) for d in range(NY) if dx or d
    ]
    others += [device(x, (z + d) % NZ, c, y) for d in range(1, NZ)]
    barrier = pltpu.get_barrier_semaphore()
    for other in others:
        pl.semaphore_signal(barrier, inc=1, device_id=other, device_id_type=MESH)

    lane = lax.broadcasted_iota(jnp.int32, (8, 128), 1)

    def note(k, found):
        chip = owners_ref[k] // 2
        spot[k] = (chip % NZ) * 16 + (chip // NZ) * 4 + (owners_ref[k] % 2) * 2 + slots_ref[k]
        return jnp.where(lane == owners_ref[k] * CAP + slots_ref[k], k, found)

    table[...] = lax.fori_loop(0, 64, note, jnp.zeros((8, 128), jnp.int32))
    lookup = pltpu.make_async_copy(table, inv, table_sem)
    lookup.start()
    lookup.wait()
    pl.semaphore_wait(barrier, len(others))
    ring = len(scratch) - OWNER_SCRATCH
    settle = reduce_part(g_ref, left_ref, right_ref, gm, a, *scratch[:ring])
    owner_part(settle, inv, spot, gm, a, out_ref, *scratch[ring:])


def step(owners, slots, grads, left_stats, right_stats):
    vm = pltpu.VMEM
    dma = pltpu.SemaphoreType.DMA
    hbm = pl.BlockSpec(memory_space=pltpu.HBM)
    smem = pl.BlockSpec(memory_space=pltpu.SMEM)
    full, half = vm((512, 512), F32), vm((512, 512), BF16)

    def boxes(count, r):
        return [vm((2, count, 16 * r + 16, 128), I16)] * 2

    ring = [
        vm((1024, 128), F32), vm((16, 128), F32), vm((2, 16, 128), F32),
        vm((8, 32, 32, 128), BF16), vm((8, 32, 32, 128), BF16),
        vm((4, 32, 64, 128), BF16), vm((4, 32, 64, 128), BF16),
        vm((32, 32, 128), F32), vm((32, 64, 128), F32),
        *boxes(7, 32), *boxes(3, 8), *boxes(3, 64), *boxes(7, 8),
        dma((2, 7)), dma((2, 7)), dma((2, 3)), dma((2, 3)),
        dma((2, 3)), dma((2, 3)), dma((2, 7)), dma((2, 7)),
        dma((8,)), dma((4,)), dma((8,)), dma((8,)), dma((4,)), dma((4,)), dma, dma, dma,
    ]
    f_parts, b_parts = len(FORWARD), len(BACK)
    part = vm((b_parts, 16, 64 // b_parts, 128), BF16)
    piece = vm((f_parts, 16, 8 // f_parts, 8, 128), F32)
    owner = [
        piece, piece,
        vm((7, 144, 128), I16), vm((2, 8, 144, 128), I16), vm((2, 8, 16, 8, 128), F32),
        full, half, half, half, half, full,
        half, half, half, half, half, half, half, half,
        vm((2, 2, 512, 512), BF16), half, half,
        part, part, vm((8, 128, 128), BF16), vm((8, 128, 128), BF16), vm((128, 8, 128), F32),
        dma((f_parts,)), dma((f_parts,)), dma((7,)), dma((7,)), dma((8,)), dma((8,)),
        dma((2,)), dma((2,)), dma((b_parts,)), dma((b_parts,)), dma((7,)), dma((7,)),
    ]
    assert len(owner) == OWNER_SCRATCH
    return pl.pallas_call(
        kernel,
        out_shape=jax.ShapeDtypeStruct((64, 8, 128), BF16),
        in_specs=[smem, smem, hbm, hbm, hbm],
        out_specs=pl.BlockSpec(memory_space=pltpu.VMEM),
        scratch_shapes=[
            vm((64, 8, 128), F32), full, vm((8, 128), jnp.int32), pltpu.SMEM((8, 128), jnp.int32),
            pltpu.SMEM((64,), jnp.int32), dma, *ring, *owner
        ],
        compiler_params=pltpu.CompilerParams(
            collective_id=0, has_side_effects=True, vmem_limit_bytes=56 * 1024 * 1024
        ),
        name="shampoo_step",
    )(owners, slots, grads, left_stats, right_stats)


def shards(grads, left_stats, right_stats, owners, slots):
    return step(owners, slots, grads, left_stats, right_stats)


def solution(mesh):
    in_specs = (
        P("dp", None, None, "mp"),
        P("dp", None, None, None),
        P("dp", None, None, None),
        P(),
        P(),
    )
    out_specs = P(None, "dp", "mp")
    return jax.shard_map(shards, mesh=mesh, in_specs=in_specs, out_specs=out_specs, check_vma=False)
```

```python
import jax
import jax.numpy as jnp
from jax import lax
from jax.experimental import pallas as pl
from jax.experimental.pallas import tpu as pltpu
from jax.sharding import PartitionSpec as P

CAP = 2
NX, NZ, NY = 4, 8, 4
AHEAD = 5
FORWARD = ((4, 5, 3, 6), (2, 7, 1, 0))
BACK = ((4, 5, 3, 6), (2, 7, 1, 0))
MESH = pl.DeviceIdType.MESH
F32 = jnp.float32
BF16 = jnp.bfloat16
I16 = jnp.int16


def place():
    dp = lax.axis_index("dp")
    chip = dp // 2
    return chip // NZ, chip % NZ, dp % 2, lax.axis_index("mp")


def device(x, z, c, y):
    return ((x * NZ + z) * 2 + c, y)


class Ring:
    def __init__(self, n, r, right, left, inbox, outbox, send, recv, local, work):
        self.n, self.r, self.to = n, r, (right, left)
        self.inbox, self.outbox, self.send, self.recv, self.local = inbox, outbox, send, recv, local
        self.stage, self.peak, self.scale = work
        self.count = n - 1
        self.group = 128 // r
        self.groups = 16 // self.group

    def copy(self, way, m):
        return pltpu.make_async_remote_copy(
            src_ref=self.outbox.at[way, m],
            dst_ref=self.inbox.at[way, m],
            send_sem=self.send.at[way, m],
            recv_sem=self.recv.at[way, m],
            device_id=self.to[way],
            device_id_type=MESH,
        )

    def open(self, way, m, slot):
        steps = self.inbox[way, m, pl.ds(16 * self.r, 16), :].astype(jnp.int32).astype(F32)
        self.scale[slot] = jnp.exp(steps * (1.0 / 128)) * (1.0 / 32760)

    def spread(self, i, slot):
        rows = [self.scale[slot, pl.ds(i * self.group + q, 1), :] for q in range(self.group)]
        return jnp.concatenate([jnp.broadcast_to(row, (self.r, 128)) for row in rows], axis=0)

    def taken(self, way, m, i, slot):
        data = self.inbox[way, m, pl.ds(pl.multiple_of(i * 128, 128), 128), :]
        return data.astype(jnp.int32).astype(F32) * self.spread(i, slot)

    def own(self, step, half, i):
        return self.local(step, half * 16 + i * self.group, self.group).reshape(128, 128)

    def emit(self, m):
        hops = self.n // 2 - (m + 1) // 2
        for way in (0, 1):
            half = way if m % 2 == 0 else 1 - way
            step = hops if way == 0 else self.n - hops
            if m >= 2:
                self.copy(way, m - 2).wait_recv()
                self.open(way, m - 2, 0)

            def add(i, _):
                value = self.own(step, half, i)
                if m >= 2:
                    value = value + self.taken(way, m - 2, i, 0)
                self.stage[pl.ds(pl.multiple_of(i * 128, 128), 128), :] = value
                size = jnp.abs(value)
                for q in range(self.group):
                    self.peak[pl.ds(i * self.group + q, 1), :] = jnp.max(
                        size[q * self.r:(q + 1) * self.r], axis=0, keepdims=True
                    )
                return 0

            lax.fori_loop(0, self.groups, add, 0)
            steps = jnp.ceil(jnp.log(jnp.maximum(self.peak[...], 1e-30)) * 128)
            self.scale[1] = jnp.exp(steps * (-1.0 / 128)) * 32760
            self.outbox[way, m, pl.ds(16 * self.r, 16), :] = steps.astype(jnp.int32).astype(I16)

            def code(i, _):
                rows = pl.ds(pl.multiple_of(i * 128, 128), 128)
                value = jnp.round(self.stage[rows, :] * self.spread(i, 1))
                self.outbox[way, m, rows, :] = value.astype(jnp.int32).astype(I16)
                return 0

            lax.fori_loop(0, self.groups, code, 0)
            self.copy(way, m).start()

    def finish(self, store):
        last = self.count - 1
        for half in (0, 1):
            first = last if half == 0 else last - 1
            second = last - 1 if half == 0 else last
            self.copy(0, first).wait_recv()
            self.copy(1, second).wait_recv()
            self.open(0, first, 0)
            self.open(1, second, 1)

            def body(i, _):
                value = self.own(0, half, i)
                value = value + self.taken(0, first, i, 0) + self.taken(1, second, i, 1)
                store(half * 16 + i * self.group, value.reshape(self.group, self.r, 128))
                return 0

            lax.fori_loop(0, self.groups, body, 0)

    def drain(self):
        for way in (0, 1):
            for m in range(self.count):
                self.copy(way, m).wait_send()


def reduce_part(
    g_ref, left_ref, right_ref, gm_ref, a,
    stage, peak, scale, own_a, got_a, own_b, got_b, sum_a, sum_b,
    az_in, az_out, ax_in, ax_out, bx_in, bx_out, bz_in, bz_out,
    az_s, az_r, ax_s, ax_r, bx_s, bx_r, bz_s, bz_r,
    load_a, load_b, swap_a_s, swap_a_r, swap_b_s, swap_b_r, stat_s, stat_r, load_sem,
):
    x, z, c, y = place()
    partner = device(x, z, 1 - c, y)
    zr, zl = device(x, (z + 1) % NZ, c, y), device(x, (z + NZ - 1) % NZ, c, y)
    xr, xl = device((x + 1) % NX, z, c, y), device((x + NX - 1) % NX, z, c, y)

    def slice_a(core, rel):
        start = core * 256 + ((z + rel) % NZ) * 32
        return g_ref.at[0, pl.ds(0, 32), pl.ds(pl.multiple_of(start, 32), 32)]

    def slice_b(core, rel):
        start = core * 256 + ((x + rel) % NX) * 64
        return g_ref.at[0, pl.ds(32, 32), pl.ds(pl.multiple_of(start, 64), 64)]

    def load(kind, rel):
        if kind == "a":
            return pltpu.make_async_copy(slice_a(c, rel), own_a.at[rel], load_a.at[rel])
        return pltpu.make_async_copy(slice_b(c, rel), own_b.at[rel], load_b.at[rel])

    def swap(kind, rel):
        source, target, s, r = (
            (slice_a(1 - c, rel), got_a, swap_a_s, swap_a_r)
            if kind == "a"
            else (slice_b(1 - c, rel), got_b, swap_b_s, swap_b_r)
        )
        return pltpu.make_async_remote_copy(
            src_ref=source, dst_ref=target.at[rel], send_sem=s.at[rel], recv_sem=r.at[rel],
            device_id=partner, device_id_type=MESH,
        )

    order = [("a", 4), ("b", 2), ("a", 3), ("a", 5), ("b", 1), ("b", 3),
             ("a", 2), ("a", 6), ("a", 1), ("a", 7), ("b", 0), ("a", 0)]
    for kind, rel in order[:AHEAD]:
        swap(kind, rel).start()
        load(kind, rel).start()
    ahead = list(order[AHEAD:])

    mine = (y // 2) == c

    def keep(source):
        return pltpu.make_async_copy(source.at[0, y % 2], a, load_sem)

    def give(source):
        return pltpu.make_async_remote_copy(
            src_ref=source.at[0, y % 2], dst_ref=a, send_sem=stat_s, recv_sem=stat_r,
            device_id=partner, device_id_type=MESH,
        )

    def statistic():
        @pl.when(mine & (c == 0))
        def _():
            keep(left_ref).start()
            give(right_ref).start()

        @pl.when(mine & (c == 1))
        def _():
            keep(right_ref).start()
            give(left_ref).start()

    def need(*pieces):
        for kind, rel in pieces:
            load(kind, rel).wait()
            swap(kind, rel).wait_recv()
            if ahead:
                swap(*ahead[0]).start()
                load(*ahead.pop(0)).start()

    def local_az(rel, block, count):
        blocks = pl.ds(block, count)
        return own_a[rel, blocks].astype(F32) + got_a[rel, blocks].astype(F32)

    def local_bx(rel, block, count):
        blocks = pl.ds(block, count)
        return own_b[rel, blocks].astype(F32) + got_b[rel, blocks].astype(F32)

    def local_ax(rel, block, count):
        return sum_a[pl.ds(block, count), pl.ds(pl.multiple_of(((x + rel) % NX) * 8, 8), 8)]

    def local_bz(rel, block, count):
        return sum_b[pl.ds(block, count), pl.ds(pl.multiple_of(((z + rel) % NZ) * 8, 8), 8)]

    work = (stage, peak, scale)
    az = Ring(NZ, 32, zr, zl, az_in, az_out, az_s, az_r, local_az, work)
    bx = Ring(NX, 64, xr, xl, bx_in, bx_out, bx_s, bx_r, local_bx, work)
    ax = Ring(NX, 8, xr, xl, ax_in, ax_out, ax_s, ax_r, local_ax, work)
    bz = Ring(NZ, 8, zr, zl, bz_in, bz_out, bz_s, bz_r, local_bz, work)

    need(("a", 4))
    az.emit(0)
    need(("b", 2))
    bx.emit(0)
    need(("a", 3), ("a", 5))
    az.emit(1)
    need(("b", 1), ("b", 3))
    bx.emit(1)
    az.emit(2)
    need(("a", 2), ("a", 6))
    az.emit(3)
    bx.emit(2)
    az.emit(4)
    need(("a", 1), ("a", 7))
    statistic()
    az.emit(5)
    az.emit(6)
    need(("b", 0), ("a", 0))

    def store_b(block, value):
        sum_b[pl.ds(block, 2)] = value

    def store_a(block, value):
        sum_a[pl.ds(block, 4)] = value

    def done_a(block, value):
        gm_ref[pl.ds(block, 16)] = value * (1.0 / 64)

    def done_b(block, value):
        gm_ref[pl.ds(32 + block, 16)] = value * (1.0 / 64)

    bx.finish(store_b)
    bz.emit(0)
    bz.emit(1)
    az.finish(store_a)
    ax.emit(0)
    ax.emit(1)
    bz.emit(2)
    bz.emit(3)
    ax.emit(2)
    bz.emit(4)
    ax.finish(done_a)
    bz.emit(5)
    bz.emit(6)
    bz.finish(done_b)
    def settle():
        for ring in (az, bx, ax, bz):
            ring.drain()
        for kind, rel in order:
            swap(kind, rel).wait_send()

        @pl.when(mine)
        def _():
            keep(left_ref).wait()
            give(left_ref).wait_send()

        @pl.when((y // 2) != c)
        def _():
            give(left_ref).wait_recv()

    return settle


def split(value):
    high = value.astype(BF16)
    return high, (value - high.astype(F32)).astype(BF16)


def dot(a, b, dims=((1,), (0,))):
    return lax.dot_general(a, b, (dims, ((), ())), preferred_element_type=F32)


def product(a, b, rows, dims=((1,), (0,)), columns=None):
    part = (rows, slice(None)) if columns is None else (slice(None), columns)
    ah, al = a[0][part], a[1][part]
    bh, bl = b[0][...], b[1][...]
    return dot(ah, bh, dims) + (dot(ah, bl, dims) + dot(al, bh, dims))


def diagonal(start, count):
    row = start + lax.broadcasted_iota(jnp.int32, (count, 512), 0)
    return row == lax.broadcasted_iota(jnp.int32, (count, 512), 1)


def tiles(body, count, init=0):
    size = 512 // count

    def step(i, carry):
        start = pl.multiple_of(i * size, size)
        return body(i, start, pl.ds(start, size), carry)

    return lax.fori_loop(0, count, step, init)


def total(value):
    return jnp.sum(jnp.sum(value, axis=0, keepdims=True), axis=1, keepdims=True)


def owner_part(
    settle, inv_ref, spot_ref, gm_ref, a, out_ref,
    outp, xb, zout, zb, hb, g, gh, gl, ah, al, a2, sh, sl, fh, fl, th, tl, qh, ql,
    roots, uh, ul, outv, wb, outw, rb, fin, norm,
    x_s, x_r, z_s, z_r, p_s, p_r, r_s, r_r, w_s, w_r, b_s, b_r,
):
    x, z, c, y = place()
    partner = device(x, z, 1 - c, y)

    def row(dx):
        return (x + dx) % NX

    def send(source, target, sems, where, to):
        return pltpu.make_async_remote_copy(
            src_ref=source, dst_ref=target, send_sem=sems[0].at[where], recv_sem=sems[1].at[where],
            device_id=to, device_id_type=MESH,
        )

    def to_plane(dx, d):
        return device(row(dx), z, c, (y + d) % NY)

    def to_z(dz):
        return device(x, (z + dz) % NZ, c, y)

    plane = sorted(
        [(dx, d) for dx in range(NX) for d in range(NY)],
        key=lambda p: -(min(p[0], NX - p[0]) + min(p[1], NY - p[1])),
    )

    def along_xy(dx, d, q):
        return send(outp.at[q, dx * NY + d], xb.at[q, x * NY + y], (x_s, x_r), q, to_plane(dx, d))

    def all_xy(q):
        others = pl.ds(0, NX * NY - 1)
        return send(outp.at[q, others], xb.at[q, others], (x_s, x_r), q, to_plane(0, 1))

    def along_z(dz):
        return send(zout.at[dz - 1], zb.at[c, z], (z_s, z_r), dz - 1, to_z(dz))

    def across(dz):
        part = zb.at[c, (z + NZ - dz) % NZ]
        return send(part, part, (p_s, p_r), dz, partner)

    def forward_xy(q):
        for dx, d in plane:
            for e, dz in enumerate(FORWARD[q]):
                there = (row(dx) * NZ + (z + dz) % NZ) * 4 + (y + d) % NY
                outp[q, dx * NY + d, e] = gm_ref[inv_ref[0, there]]
            if dx or d:
                along_xy(dx, d, q).start()
            else:
                xb[q, x * NY + y] = outp[q, 0]

    def forward_z(q):
        all_xy(q).wait_recv()
        for e, dz in enumerate(FORWARD[q]):
            value = xb[q, :, e].reshape(128, 128)
            peak = jnp.max(jnp.abs(value), axis=0, keepdims=True)
            steps = jnp.ceil(jnp.log(jnp.maximum(peak, 1e-30)) * 128)
            value = jnp.round(value * (jnp.exp(steps * (-1.0 / 128)) * 32760))
            value = jnp.concatenate([value, jnp.broadcast_to(steps, (16, 128))], axis=0)
            value = value.astype(jnp.int32).astype(I16)
            if dz:
                zout[dz - 1] = value
                along_z(dz).start()
            else:
                zb[c, z] = value
                across(0).start()

    forward_xy(0)
    for q in range(1, len(FORWARD)):
        forward_xy(q)
        forward_z(q - 1)
    forward_z(len(FORWARD) - 1)

    def decode(core, zz):
        steps = zb[core, zz, pl.ds(128, 16), :].astype(jnp.int32).astype(F32)[:1]
        scale = jnp.exp(steps * (1.0 / 128)) * (1.0 / 32760)
        value = zb[core, zz, pl.ds(0, 128), :].astype(jnp.int32).astype(F32) * scale
        hb[core, zz] = value.reshape(16, 8, 128)

    decode(c, z)
    settle()
    for dz in (1, 7, 2, 6, 3, 5, 4):
        along_z(dz).wait_recv()
        across(dz).start()
        decode(c, (z + NZ - dz) % NZ)
    for dz in (0, 1, 7, 2, 6, 3, 5, 4):
        across(dz).wait_recv()
        decode(1 - c, (z + NZ - dz) % NZ)

    early = inv_ref[0, (x * NZ + z) * 4 + y] < 32

    def assemble(p, _):
        piece = jnp.where(early, p, (p % NZ) * NX + p // NZ) * 4
        for core in range(2):
            start = pl.multiple_of(core * 256 + p * 8, 8)
            for yy in range(NY):
                g[pl.ds(start, 8), yy * 128:yy * 128 + 128] = hb[core, piece // 16, piece % 16 + yy]
        return 0

    lax.fori_loop(0, 32, assemble, 0)

    def split_g(i, start, rows, squares):
        value = g[rows, :]
        gh[rows, :], gl[rows, :] = split(value)
        return squares + total(value * value)

    zero = jnp.zeros((1, 1), F32)
    grad_squares = tiles(split_g, 4, zero)

    pair_g = (gh, gl)

    def rows_of(i):
        return pl.ds(i * 256, 256)

    @pl.when(c == 0)
    def _():
        for i in range(2):
            a[rows_of(i), :] = 0.95 * a[rows_of(i), :] + product(pair_g, pair_g, rows_of(i), ((1,), (1,)))

    @pl.when(c == 1)
    def _():
        for i in range(2):
            a[rows_of(i), :] = 0.95 * a[rows_of(i), :] + product(
                pair_g, pair_g, None, ((0,), (0,)), columns=rows_of(i)
            )

    corner = diagonal(0, 128)[:, :128]
    size = zero
    for i in range(4):
        part = slice(i * 128, i * 128 + 128)
        size = size + total(jnp.where(corner, a[part, part], 0.0))
    size = size * (1.0 / 512)
    scale = 1.0 / size

    def split_a(i, start, rows, carry):
        value = a[rows, :] * scale
        a[rows, :] = value
        ah[rows, :], al[rows, :] = split(value)
        return carry

    tiles(split_a, 4)
    pair_a = (ah, al)

    def square(i, start, rows, carry):
        a2[rows, :] = product(pair_a, pair_a, rows)
        return carry

    tiles(square, 1)

    def unit(image):
        return image / jnp.sqrt(total(image * image))

    vector = jnp.full((1, 512), 512 ** (-0.5), F32)
    vector = unit(jnp.sum(a2[...] * vector, axis=1, keepdims=True))
    vector = unit(jnp.sum(a2[...] * vector, axis=0, keepdims=True))
    vector = unit(jnp.sum(a2[...] * vector, axis=1, keepdims=True))
    image = jnp.sum(a[...] * vector, axis=0, keepdims=True)
    flat = jnp.concatenate(
        [
            jnp.sum(jnp.where(corner, vector[i * 128:i * 128 + 128], 0.0), axis=0, keepdims=True)
            for i in range(4)
        ],
        axis=1,
    )
    largest = total(flat * image)
    factor = 2.5 / largest
    fourth = jnp.sqrt(jnp.sqrt(factor * scale))

    def first_terms(i, start, rows, carry):
        eye = jnp.where(diagonal(start, 128), 1.0, 0.0)
        value = a[rows, :] * factor
        qh[rows, :], ql[rows, :] = split(1.25 * eye - 0.25 * value)
        squared = (25.0 / 16) * eye - (10.0 / 16) * value + (factor * factor * (1.0 / 16)) * a2[rows, :]
        sh[rows, :], sl[rows, :] = split(squared)
        return carry

    tiles(first_terms, 4)

    def power_four(i, start, rows, carry):
        fh[rows, :], fl[rows, :] = split(product((sh, sl), (sh, sl), rows))
        return carry

    tiles(power_four, 1)

    def second_term(i, start, rows, carry):
        value = product((fh, fl), pair_a, rows) * (0.25 * factor)
        th[rows, :], tl[rows, :] = split(jnp.where(diagonal(start, 512), 1.25, 0.0) - value)
        return carry

    tiles(second_term, 1)

    def send_root(i):
        part = roots.at[c, :, pl.ds(i * 256, 256)]
        return pltpu.make_async_remote_copy(
            src_ref=part, dst_ref=part, send_sem=r_s.at[i], recv_sem=r_r.at[i],
            device_id=partner, device_id_type=MESH,
        )

    for i in range(2):
        rows = rows_of(i)
        high, low = split(product((qh, ql), (th, tl), rows) * fourth)
        roots[c, 0, rows, :] = high
        roots[c, 1, rows, :] = low
        send_root(i).start()

    pair_l = (roots.at[0, 0], roots.at[0, 1])
    pair_r = (roots.at[1, 0], roots.at[1, 1])
    pair_u = (uh, ul)

    def middle(one, two):
        def body(i, start, rows, carry):
            uh[rows, :], ul[rows, :] = split(product(one, two, rows))
            return carry

        tiles(body, 1)

    @pl.when(c == 0)
    def _():
        middle(pair_l, pair_g)

    @pl.when(c == 1)
    def _():
        middle(pair_g, pair_r)

    for i in range(2):
        send_root(i).wait_recv()

    def outer(one, two):
        def body(i, start, rows, carry):
            value = product(one, two, rows)
            a2[rows, :] = value
            norm[...] = total(value * value)
            return carry

        tiles(body, 1)

    @pl.when(c == 0)
    def _():
        outer(pair_u, pair_r)

    @pl.when(c == 1)
    def _():
        outer(pair_l, pair_u)

    ratio = jnp.sqrt((grad_squares + 1e-06) / (norm[...] + 1e-06))

    def back_xy(dx, d, q):
        return send(outv.at[q, dx * NY + d], wb.at[q, x * NY + y], (w_s, w_r), q, to_plane(dx, d))

    def all_back(q):
        others = pl.ds(0, NX * NY - 1)
        return send(outv.at[q, others], wb.at[q, others], (w_s, w_r), q, to_plane(0, 1))

    def back_z(dz):
        return send(outw.at[dz], rb.at[z], (b_s, b_r), dz - 1, to_z(dz))

    def return_xy(q):
        for dx, d in plane:
            column = pl.ds(pl.multiple_of(((y + d) % NY) * 128, 128), 128)
            two = [
                a2[pl.ds(pl.multiple_of((row(dx) * NZ + (z + dz) % NZ) * 16 + c * 8, 8), 8), column]
                for dz in BACK[q]
            ]
            outv[q, dx * NY + d] = (jnp.concatenate(two, axis=0) * ratio).astype(BF16)
            if dx or d:
                back_xy(dx, d, q).start()
            else:
                wb[q, x * NY + y] = outv[q, 0]

    def return_z(q):
        all_back(q).wait_recv()
        value = wb[q].astype(F32).reshape(16, len(BACK[0]), 8, 128)
        for e, dz in enumerate(BACK[q]):
            part = value[:, e].reshape(128, 128).astype(BF16)
            if dz:
                outw[dz] = part
                back_z(dz).start()
            else:
                rb[z] = part

    return_xy(0)
    for q in range(1, len(BACK)):
        return_xy(q)
        return_z(q - 1)
    return_z(len(BACK) - 1)
    for q in range(len(FORWARD)):
        all_xy(q).wait_send()
    for dz in range(NZ):
        if dz:
            along_z(dz).wait_send()
        across(dz).wait_send()
    for i in range(2):
        send_root(i).wait_send()
    def unpack(zz):
        fin[pl.ds(zz * 16, 16)] = rb[zz].astype(F32).reshape(16, 8, 128)

    unpack(z)
    for dz in (1, 7, 2, 6, 3, 5, 4):
        back_z(dz).wait_recv()
        unpack((z + NZ - dz) % NZ)

    def pick(i, _):
        for k in range(8):
            out_ref[i * 8 + k] = fin[spot_ref[i * 8 + k]].astype(BF16)
        return 0

    lax.fori_loop(0, 8, pick, 0)

    for q in range(len(BACK)):
        all_back(q).wait_send()
    for dz in range(1, NZ):
        back_z(dz).wait_send()


OWNER_SCRATCH = 40


def kernel(owners_ref, slots_ref, g_ref, left_ref, right_ref, out_ref, gm, a, table, inv, spot, table_sem, *scratch):
    x, z, c, y = place()
    others = [device(x, z, 1 - c, y)]
    others += [
        device((x + dx) % NX, z, c, (y + d) % NY) for dx in range(NX) for d in range(NY) if dx or d
    ]
    others += [device(x, (z + d) % NZ, c, y) for d in range(1, NZ)]
    barrier = pltpu.get_barrier_semaphore()
    for other in others:
        pl.semaphore_signal(barrier, inc=1, device_id=other, device_id_type=MESH)

    lane = lax.broadcasted_iota(jnp.int32, (8, 128), 1)

    def note(k, found):
        chip = owners_ref[k] // 2
        spot[k] = (chip % NZ) * 16 + (chip // NZ) * 4 + (owners_ref[k] % 2) * 2 + slots_ref[k]
        return jnp.where(lane == owners_ref[k] * CAP + slots_ref[k], k, found)

    table[...] = lax.fori_loop(0, 64, note, jnp.zeros((8, 128), jnp.int32))
    lookup = pltpu.make_async_copy(table, inv, table_sem)
    lookup.start()
    lookup.wait()
    pl.semaphore_wait(barrier, len(others))
    ring = len(scratch) - OWNER_SCRATCH
    settle = reduce_part(g_ref, left_ref, right_ref, gm, a, *scratch[:ring])
    owner_part(settle, inv, spot, gm, a, out_ref, *scratch[ring:])


def step(owners, slots, grads, left_stats, right_stats):
    vm = pltpu.VMEM
    dma = pltpu.SemaphoreType.DMA
    hbm = pl.BlockSpec(memory_space=pltpu.HBM)
    smem = pl.BlockSpec(memory_space=pltpu.SMEM)
    full, half = vm((512, 512), F32), vm((512, 512), BF16)

    def boxes(count, r):
        return [vm((2, count, 16 * r + 16, 128), I16)] * 2

    ring = [
        vm((1024, 128), F32), vm((16, 128), F32), vm((2, 16, 128), F32),
        vm((8, 32, 32, 128), BF16), vm((8, 32, 32, 128), BF16),
        vm((4, 32, 64, 128), BF16), vm((4, 32, 64, 128), BF16),
        vm((32, 32, 128), F32), vm((32, 64, 128), F32),
        *boxes(7, 32), *boxes(3, 8), *boxes(3, 64), *boxes(7, 8),
        dma((2, 7)), dma((2, 7)), dma((2, 3)), dma((2, 3)),
        dma((2, 3)), dma((2, 3)), dma((2, 7)), dma((2, 7)),
        dma((8,)), dma((4,)), dma((8,)), dma((8,)), dma((4,)), dma((4,)), dma, dma, dma,
    ]
    f_parts, b_parts = len(FORWARD), len(BACK)
    part = vm((b_parts, 16, 64 // b_parts, 128), BF16)
    piece = vm((f_parts, 16, 8 // f_parts, 8, 128), F32)
    owner = [
        piece, piece,
        vm((7, 144, 128), I16), vm((2, 8, 144, 128), I16), vm((2, 8, 16, 8, 128), F32),
        full, half, half, half, half, full,
        half, half, half, half, half, half, half, half,
        vm((2, 2, 512, 512), BF16), half, half,
        part, part, vm((8, 128, 128), BF16), vm((8, 128, 128), BF16), vm((128, 8, 128), F32), vm((1, 1), F32),
        dma((f_parts,)), dma((f_parts,)), dma((7,)), dma((7,)), dma((8,)), dma((8,)),
        dma((2,)), dma((2,)), dma((b_parts,)), dma((b_parts,)), dma((7,)), dma((7,)),
    ]
    assert len(owner) == OWNER_SCRATCH
    return pl.pallas_call(
        kernel,
        out_shape=jax.ShapeDtypeStruct((64, 8, 128), BF16),
        in_specs=[smem, smem, hbm, hbm, hbm],
        out_specs=pl.BlockSpec(memory_space=pltpu.VMEM),
        scratch_shapes=[
            vm((64, 8, 128), F32), full, vm((8, 128), jnp.int32), pltpu.SMEM((8, 128), jnp.int32),
            pltpu.SMEM((64,), jnp.int32), dma, *ring, *owner
        ],
        compiler_params=pltpu.CompilerParams(
            collective_id=0, has_side_effects=True, vmem_limit_bytes=56 * 1024 * 1024
        ),
        name="shampoo_step",
    )(owners, slots, grads, left_stats, right_stats)


def shards(grads, left_stats, right_stats, owners, slots):
    return step(owners, slots, grads, left_stats, right_stats)


def solution(mesh):
    in_specs = (
        P("dp", None, None, "mp"),
        P("dp", None, None, None),
        P("dp", None, None, None),
        P(),
        P(),
    )
    out_specs = P(None, "dp", "mp")
    return jax.shard_map(shards, mesh=mesh, in_specs=in_specs, out_specs=out_specs, check_vma=False)
```

```python
import jax
import jax.numpy as jnp
from jax import lax
from jax.experimental import pallas as pl
from jax.experimental.pallas import tpu as pltpu
from jax.sharding import PartitionSpec as P

CAP = 2
NX, NZ, NY = 4, 8, 4
AHEAD = 5
FORWARD = ((4, 5, 3, 6), (2, 7, 1, 0))
BACK = ((4, 5, 3, 6), (2, 7, 1, 0))
MESH = pl.DeviceIdType.MESH
F32 = jnp.float32
BF16 = jnp.bfloat16
I16 = jnp.int16


def place():
    dp = lax.axis_index("dp")
    chip = dp // 2
    return chip // NZ, chip % NZ, dp % 2, lax.axis_index("mp")


def device(x, z, c, y):
    return ((x * NZ + z) * 2 + c, y)


class Ring:
    def __init__(self, n, r, right, left, inbox, outbox, send, recv, local, work):
        self.n, self.r, self.to = n, r, (right, left)
        self.inbox, self.outbox, self.send, self.recv, self.local = inbox, outbox, send, recv, local
        self.stage, self.peak, self.scale = work
        self.count = n - 1
        self.group = 128 // r
        self.groups = 16 // self.group

    def copy(self, way, m):
        return pltpu.make_async_remote_copy(
            src_ref=self.outbox.at[way, m],
            dst_ref=self.inbox.at[way, m],
            send_sem=self.send.at[way, m],
            recv_sem=self.recv.at[way, m],
            device_id=self.to[way],
            device_id_type=MESH,
        )

    def open(self, way, m, slot):
        steps = self.inbox[way, m, pl.ds(16 * self.r, 16), :].astype(jnp.int32).astype(F32)
        self.scale[slot] = jnp.exp(steps * (1.0 / 128)) * (1.0 / 32760)

    def spread(self, i, slot):
        rows = [self.scale[slot, pl.ds(i * self.group + q, 1), :] for q in range(self.group)]
        return jnp.concatenate([jnp.broadcast_to(row, (self.r, 128)) for row in rows], axis=0)

    def taken(self, way, m, i, slot):
        data = self.inbox[way, m, pl.ds(pl.multiple_of(i * 128, 128), 128), :]
        return data.astype(jnp.int32).astype(F32) * self.spread(i, slot)

    def own(self, step, half, i):
        return self.local(step, half * 16 + i * self.group, self.group).reshape(128, 128)

    def emit(self, m):
        hops = self.n // 2 - (m + 1) // 2
        for way in (0, 1):
            half = way if m % 2 == 0 else 1 - way
            step = hops if way == 0 else self.n - hops
            if m >= 2:
                self.copy(way, m - 2).wait_recv()
                self.open(way, m - 2, 0)

            def add(i, _):
                value = self.own(step, half, i)
                if m >= 2:
                    value = value + self.taken(way, m - 2, i, 0)
                self.stage[pl.ds(pl.multiple_of(i * 128, 128), 128), :] = value
                size = jnp.abs(value)
                for q in range(self.group):
                    self.peak[pl.ds(i * self.group + q, 1), :] = jnp.max(
                        size[q * self.r:(q + 1) * self.r], axis=0, keepdims=True
                    )
                return 0

            lax.fori_loop(0, self.groups, add, 0)
            steps = jnp.ceil(jnp.log(jnp.maximum(self.peak[...], 1e-30)) * 128)
            self.scale[1] = jnp.exp(steps * (-1.0 / 128)) * 32760
            self.outbox[way, m, pl.ds(16 * self.r, 16), :] = steps.astype(jnp.int32).astype(I16)

            def code(i, _):
                rows = pl.ds(pl.multiple_of(i * 128, 128), 128)
                value = jnp.round(self.stage[rows, :] * self.spread(i, 1))
                self.outbox[way, m, rows, :] = value.astype(jnp.int32).astype(I16)
                return 0

            lax.fori_loop(0, self.groups, code, 0)
            self.copy(way, m).start()

    def finish(self, store):
        last = self.count - 1
        for half in (0, 1):
            first = last if half == 0 else last - 1
            second = last - 1 if half == 0 else last
            self.copy(0, first).wait_recv()
            self.copy(1, second).wait_recv()
            self.open(0, first, 0)
            self.open(1, second, 1)

            def body(i, _):
                value = self.own(0, half, i)
                value = value + self.taken(0, first, i, 0) + self.taken(1, second, i, 1)
                store(half * 16 + i * self.group, value.reshape(self.group, self.r, 128))
                return 0

            lax.fori_loop(0, self.groups, body, 0)

    def drain(self):
        for way in (0, 1):
            for m in range(self.count):
                self.copy(way, m).wait_send()


def reduce_part(
    g_ref, left_ref, right_ref, gm_ref, a,
    stage, peak, scale, own_a, got_a, own_b, got_b, sum_a, sum_b,
    az_in, az_out, ax_in, ax_out, bx_in, bx_out, bz_in, bz_out,
    az_s, az_r, ax_s, ax_r, bx_s, bx_r, bz_s, bz_r,
    load_a, load_b, swap_a_s, swap_a_r, swap_b_s, swap_b_r, stat_s, stat_r, load_sem,
):
    x, z, c, y = place()
    partner = device(x, z, 1 - c, y)
    zr, zl = device(x, (z + 1) % NZ, c, y), device(x, (z + NZ - 1) % NZ, c, y)
    xr, xl = device((x + 1) % NX, z, c, y), device((x + NX - 1) % NX, z, c, y)

    def slice_a(core, rel):
        start = core * 256 + ((z + rel) % NZ) * 32
        return g_ref.at[0, pl.ds(0, 32), pl.ds(pl.multiple_of(start, 32), 32)]

    def slice_b(core, rel):
        start = core * 256 + ((x + rel) % NX) * 64
        return g_ref.at[0, pl.ds(32, 32), pl.ds(pl.multiple_of(start, 64), 64)]

    def load(kind, rel):
        if kind == "a":
            return pltpu.make_async_copy(slice_a(c, rel), own_a.at[rel], load_a.at[rel])
        return pltpu.make_async_copy(slice_b(c, rel), own_b.at[rel], load_b.at[rel])

    def swap(kind, rel):
        source, target, s, r = (
            (slice_a(1 - c, rel), got_a, swap_a_s, swap_a_r)
            if kind == "a"
            else (slice_b(1 - c, rel), got_b, swap_b_s, swap_b_r)
        )
        return pltpu.make_async_remote_copy(
            src_ref=source, dst_ref=target.at[rel], send_sem=s.at[rel], recv_sem=r.at[rel],
            device_id=partner, device_id_type=MESH,
        )

    order = [("a", 4), ("b", 2), ("a", 3), ("a", 5), ("b", 1), ("b", 3),
             ("a", 2), ("a", 6), ("a", 1), ("a", 7), ("b", 0), ("a", 0)]
    for kind, rel in order[:AHEAD]:
        swap(kind, rel).start()
        load(kind, rel).start()
    ahead = list(order[AHEAD:])

    mine = (y // 2) == c

    def keep(source):
        return pltpu.make_async_copy(source.at[0, y % 2], a, load_sem)

    def give(source):
        return pltpu.make_async_remote_copy(
            src_ref=source.at[0, y % 2], dst_ref=a, send_sem=stat_s, recv_sem=stat_r,
            device_id=partner, device_id_type=MESH,
        )

    def statistic():
        @pl.when(mine & (c == 0))
        def _():
            keep(left_ref).start()
            give(right_ref).start()

        @pl.when(mine & (c == 1))
        def _():
            keep(right_ref).start()
            give(left_ref).start()

    def need(*pieces):
        for kind, rel in pieces:
            load(kind, rel).wait()
            swap(kind, rel).wait_recv()
            if ahead:
                swap(*ahead[0]).start()
                load(*ahead.pop(0)).start()

    def local_az(rel, block, count):
        blocks = pl.ds(block, count)
        return own_a[rel, blocks].astype(F32) + got_a[rel, blocks].astype(F32)

    def local_bx(rel, block, count):
        blocks = pl.ds(block, count)
        return own_b[rel, blocks].astype(F32) + got_b[rel, blocks].astype(F32)

    def local_ax(rel, block, count):
        return sum_a[pl.ds(block, count), pl.ds(pl.multiple_of(((x + rel) % NX) * 8, 8), 8)]

    def local_bz(rel, block, count):
        return sum_b[pl.ds(block, count), pl.ds(pl.multiple_of(((z + rel) % NZ) * 8, 8), 8)]

    work = (stage, peak, scale)
    az = Ring(NZ, 32, zr, zl, az_in, az_out, az_s, az_r, local_az, work)
    bx = Ring(NX, 64, xr, xl, bx_in, bx_out, bx_s, bx_r, local_bx, work)
    ax = Ring(NX, 8, xr, xl, ax_in, ax_out, ax_s, ax_r, local_ax, work)
    bz = Ring(NZ, 8, zr, zl, bz_in, bz_out, bz_s, bz_r, local_bz, work)

    need(("a", 4))
    az.emit(0)
    need(("b", 2))
    bx.emit(0)
    need(("a", 3), ("a", 5))
    az.emit(1)
    need(("b", 1), ("b", 3))
    bx.emit(1)
    az.emit(2)
    need(("a", 2), ("a", 6))
    az.emit(3)
    bx.emit(2)
    az.emit(4)
    need(("a", 1), ("a", 7))
    statistic()
    az.emit(5)
    az.emit(6)
    need(("b", 0), ("a", 0))

    def store_b(block, value):
        sum_b[pl.ds(block, 2)] = value

    def store_a(block, value):
        sum_a[pl.ds(block, 4)] = value

    def done_a(block, value):
        gm_ref[pl.ds(block, 16)] = value * (1.0 / 64)

    def done_b(block, value):
        gm_ref[pl.ds(32 + block, 16)] = value * (1.0 / 64)

    bx.finish(store_b)
    bz.emit(0)
    bz.emit(1)
    az.finish(store_a)
    ax.emit(0)
    ax.emit(1)
    bz.emit(2)
    bz.emit(3)
    ax.emit(2)
    bz.emit(4)
    ax.finish(done_a)
    bz.emit(5)
    bz.emit(6)
    bz.finish(done_b)
    def settle():
        for ring in (az, bx, ax, bz):
            ring.drain()
        for kind, rel in order:
            swap(kind, rel).wait_send()

        @pl.when(mine)
        def _():
            keep(left_ref).wait()
            give(left_ref).wait_send()

        @pl.when((y // 2) != c)
        def _():
            give(left_ref).wait_recv()

    return settle


def split(value):
    high = value.astype(BF16)
    return high, (value - high.astype(F32)).astype(BF16)


def dot(a, b, dims=((1,), (0,))):
    return lax.dot_general(a, b, (dims, ((), ())), preferred_element_type=F32)


def product(a, b, rows, dims=((1,), (0,)), columns=None):
    part = (rows, slice(None)) if columns is None else (slice(None), columns)
    ah, al = a[0][part], a[1][part]
    bh, bl = b[0][...], b[1][...]
    return dot(ah, bh, dims) + (dot(ah, bl, dims) + dot(al, bh, dims))


def diagonal(start, count):
    row = start + lax.broadcasted_iota(jnp.int32, (count, 512), 0)
    return row == lax.broadcasted_iota(jnp.int32, (count, 512), 1)


def tiles(body, count, init=0):
    size = 512 // count

    def step(i, carry):
        start = pl.multiple_of(i * size, size)
        return body(i, start, pl.ds(start, size), carry)

    return lax.fori_loop(0, count, step, init)


def total(value):
    return jnp.sum(jnp.sum(value, axis=0, keepdims=True), axis=1, keepdims=True)


def owner_part(
    settle, inv_ref, spot_ref, gm_ref, a, out_ref,
    outp, xb, zout, zb, hb, g, gh, gl, ah, al, a2, sh, sl, fh, fl, th, tl, qh, ql,
    roots, uh, ul, outv, wb, outw, rb, fin, norm,
    x_s, x_r, z_s, z_r, p_s, p_r, r_s, r_r, w_s, w_r, b_s, b_r,
):
    x, z, c, y = place()
    partner = device(x, z, 1 - c, y)

    def row(dx):
        return (x + dx) % NX

    def send(source, target, sems, where, to):
        return pltpu.make_async_remote_copy(
            src_ref=source, dst_ref=target, send_sem=sems[0].at[where], recv_sem=sems[1].at[where],
            device_id=to, device_id_type=MESH,
        )

    def to_plane(dx, d):
        return device(row(dx), z, c, (y + d) % NY)

    def to_z(dz):
        return device(x, (z + dz) % NZ, c, y)

    plane = sorted(
        [(dx, d) for dx in range(NX) for d in range(NY)],
        key=lambda p: -(min(p[0], NX - p[0]) + min(p[1], NY - p[1])),
    )

    def along_xy(dx, d, q):
        return send(outp.at[q, dx * NY + d], xb.at[q, x * NY + y], (x_s, x_r), q, to_plane(dx, d))

    def all_xy(q):
        others = pl.ds(0, NX * NY - 1)
        return send(outp.at[q, others], xb.at[q, others], (x_s, x_r), q, to_plane(0, 1))

    def along_z(dz):
        return send(zout.at[dz - 1], zb.at[c, z], (z_s, z_r), dz - 1, to_z(dz))

    def across(dz):
        part = zb.at[c, (z + NZ - dz) % NZ]
        return send(part, part, (p_s, p_r), dz, partner)

    def forward_xy(q):
        for dx, d in plane:
            for e, dz in enumerate(FORWARD[q]):
                there = (row(dx) * NZ + (z + dz) % NZ) * 4 + (y + d) % NY
                outp[q, dx * NY + d, e] = gm_ref[inv_ref[0, there]]
            if dx or d:
                along_xy(dx, d, q).start()
            else:
                xb[q, x * NY + y] = outp[q, 0]

    def forward_z(q):
        all_xy(q).wait_recv()
        for e, dz in enumerate(FORWARD[q]):
            value = xb[q, :, e].reshape(128, 128)
            peak = jnp.max(jnp.abs(value), axis=0, keepdims=True)
            steps = jnp.ceil(jnp.log(jnp.maximum(peak, 1e-30)) * 128)
            value = jnp.round(value * (jnp.exp(steps * (-1.0 / 128)) * 32760))
            value = jnp.concatenate([value, jnp.broadcast_to(steps, (16, 128))], axis=0)
            value = value.astype(jnp.int32).astype(I16)
            if dz:
                zout[dz - 1] = value
                along_z(dz).start()
            else:
                zb[c, z] = value
                across(0).start()

    forward_xy(0)
    for q in range(1, len(FORWARD)):
        forward_xy(q)
        forward_z(q - 1)
    forward_z(len(FORWARD) - 1)

    def decode(core, zz):
        steps = zb[core, zz, pl.ds(128, 16), :].astype(jnp.int32).astype(F32)[:1]
        scale = jnp.exp(steps * (1.0 / 128)) * (1.0 / 32760)
        value = zb[core, zz, pl.ds(0, 128), :].astype(jnp.int32).astype(F32) * scale
        hb[core, zz] = value.reshape(16, 8, 128)

    decode(c, z)
    settle()
    for dz in (1, 7, 2, 6, 3, 5, 4):
        along_z(dz).wait_recv()
        across(dz).start()
        decode(c, (z + NZ - dz) % NZ)
    for dz in (0, 1, 7, 2, 6, 3, 5, 4):
        across(dz).wait_recv()
        decode(1 - c, (z + NZ - dz) % NZ)

    early = inv_ref[0, (x * NZ + z) * 4 + y] < 32

    def assemble(p, _):
        piece = jnp.where(early, p, (p % NZ) * NX + p // NZ) * 4
        for core in range(2):
            start = pl.multiple_of(core * 256 + p * 8, 8)
            for yy in range(NY):
                g[pl.ds(start, 8), yy * 128:yy * 128 + 128] = hb[core, piece // 16, piece % 16 + yy]
        return 0

    lax.fori_loop(0, 32, assemble, 0, unroll=8)

    def split_g(i, start, rows, squares):
        value = g[rows, :]
        gh[rows, :], gl[rows, :] = split(value)
        return squares + total(value * value)

    zero = jnp.zeros((1, 1), F32)
    grad_squares = tiles(split_g, 4, zero)

    pair_g = (gh, gl)

    def rows_of(i):
        return pl.ds(i * 256, 256)

    @pl.when(c == 0)
    def _():
        for i in range(2):
            a[rows_of(i), :] = 0.95 * a[rows_of(i), :] + product(pair_g, pair_g, rows_of(i), ((1,), (1,)))

    @pl.when(c == 1)
    def _():
        for i in range(2):
            a[rows_of(i), :] = 0.95 * a[rows_of(i), :] + product(
                pair_g, pair_g, None, ((0,), (0,)), columns=rows_of(i)
            )

    corner = diagonal(0, 128)[:, :128]
    size = zero
    for i in range(4):
        part = slice(i * 128, i * 128 + 128)
        size = size + total(jnp.where(corner, a[part, part], 0.0))
    size = size * (1.0 / 512)
    scale = 1.0 / size

    def split_a(i, start, rows, carry):
        value = a[rows, :] * scale
        a[rows, :] = value
        ah[rows, :], al[rows, :] = split(value)
        return carry

    tiles(split_a, 4)
    pair_a = (ah, al)

    def square(i, start, rows, carry):
        a2[rows, :] = product(pair_a, pair_a, rows)
        return carry

    tiles(square, 1)

    def unit(image):
        return image / jnp.sqrt(total(image * image))

    vector = jnp.full((1, 512), 512 ** (-0.5), F32)
    vector = unit(jnp.sum(a2[...] * vector, axis=1, keepdims=True))
    vector = unit(jnp.sum(a2[...] * vector, axis=0, keepdims=True))
    vector = unit(jnp.sum(a2[...] * vector, axis=1, keepdims=True))
    image = jnp.sum(a[...] * vector, axis=0, keepdims=True)
    flat = jnp.concatenate(
        [
            jnp.sum(jnp.where(corner, vector[i * 128:i * 128 + 128], 0.0), axis=0, keepdims=True)
            for i in range(4)
        ],
        axis=1,
    )
    largest = total(flat * image)
    factor = 2.5 / largest
    fourth = jnp.sqrt(jnp.sqrt(factor * scale))

    def first_terms(i, start, rows, carry):
        eye = jnp.where(diagonal(start, 128), 1.0, 0.0)
        value = a[rows, :] * factor
        qh[rows, :], ql[rows, :] = split(1.25 * eye - 0.25 * value)
        squared = (25.0 / 16) * eye - (10.0 / 16) * value + (factor * factor * (1.0 / 16)) * a2[rows, :]
        sh[rows, :], sl[rows, :] = split(squared)
        return carry

    tiles(first_terms, 4)

    def power_four(i, start, rows, carry):
        fh[rows, :], fl[rows, :] = split(product((sh, sl), (sh, sl), rows))
        return carry

    tiles(power_four, 1)

    def second_term(i, start, rows, carry):
        value = product((fh, fl), pair_a, rows) * (0.25 * factor)
        th[rows, :], tl[rows, :] = split(jnp.where(diagonal(start, 512), 1.25, 0.0) - value)
        return carry

    tiles(second_term, 1)

    def send_root(i):
        part = roots.at[c, :, pl.ds(i * 256, 256)]
        return pltpu.make_async_remote_copy(
            src_ref=part, dst_ref=part, send_sem=r_s.at[i], recv_sem=r_r.at[i],
            device_id=partner, device_id_type=MESH,
        )

    for i in range(2):
        rows = rows_of(i)
        high, low = split(product((qh, ql), (th, tl), rows) * fourth)
        roots[c, 0, rows, :] = high
        roots[c, 1, rows, :] = low
        send_root(i).start()

    pair_l = (roots.at[0, 0], roots.at[0, 1])
    pair_r = (roots.at[1, 0], roots.at[1, 1])
    pair_u = (uh, ul)

    def middle(one, two):
        def body(i, start, rows, carry):
            uh[rows, :], ul[rows, :] = split(product(one, two, rows))
            return carry

        tiles(body, 1)

    @pl.when(c == 0)
    def _():
        middle(pair_l, pair_g)

    @pl.when(c == 1)
    def _():
        middle(pair_g, pair_r)

    for i in range(2):
        send_root(i).wait_recv()

    def outer(one, two):
        def body(i, start, rows, carry):
            value = product(one, two, rows)
            a2[rows, :] = value
            norm[...] = total(value * value)
            return carry

        tiles(body, 1)

    @pl.when(c == 0)
    def _():
        outer(pair_u, pair_r)

    @pl.when(c == 1)
    def _():
        outer(pair_l, pair_u)

    ratio = jnp.sqrt((grad_squares + 1e-06) / (norm[...] + 1e-06))

    def back_xy(dx, d, q):
        return send(outv.at[q, dx * NY + d], wb.at[q, x * NY + y], (w_s, w_r), q, to_plane(dx, d))

    def all_back(q):
        others = pl.ds(0, NX * NY - 1)
        return send(outv.at[q, others], wb.at[q, others], (w_s, w_r), q, to_plane(0, 1))

    def back_z(dz):
        return send(outw.at[dz], rb.at[z], (b_s, b_r), dz - 1, to_z(dz))

    def return_xy(q):
        for dx, d in plane:
            column = pl.ds(pl.multiple_of(((y + d) % NY) * 128, 128), 128)
            two = [
                a2[pl.ds(pl.multiple_of((row(dx) * NZ + (z + dz) % NZ) * 16 + c * 8, 8), 8), column]
                for dz in BACK[q]
            ]
            outv[q, dx * NY + d] = (jnp.concatenate(two, axis=0) * ratio).astype(BF16)
            if dx or d:
                back_xy(dx, d, q).start()
            else:
                wb[q, x * NY + y] = outv[q, 0]

    def return_z(q):
        all_back(q).wait_recv()
        value = wb[q].astype(F32).reshape(16, len(BACK[0]), 8, 128)
        for e, dz in enumerate(BACK[q]):
            part = value[:, e].reshape(128, 128).astype(BF16)
            if dz:
                outw[dz] = part
                back_z(dz).start()
            else:
                rb[z] = part

    return_xy(0)
    for q in range(1, len(BACK)):
        return_xy(q)
        return_z(q - 1)
    return_z(len(BACK) - 1)
    for q in range(len(FORWARD)):
        all_xy(q).wait_send()
    for dz in range(NZ):
        if dz:
            along_z(dz).wait_send()
        across(dz).wait_send()
    for i in range(2):
        send_root(i).wait_send()
    def unpack(zz):
        fin[pl.ds(zz * 16, 16)] = rb[zz].astype(F32).reshape(16, 8, 128)

    unpack(z)
    for dz in (1, 7, 2, 6, 3, 5, 4):
        back_z(dz).wait_recv()
        unpack((z + NZ - dz) % NZ)

    def pick(i, _):
        for k in range(8):
            out_ref[i * 8 + k] = fin[spot_ref[i * 8 + k]].astype(BF16)
        return 0

    lax.fori_loop(0, 8, pick, 0)

    for q in range(len(BACK)):
        all_back(q).wait_send()
    for dz in range(1, NZ):
        back_z(dz).wait_send()


OWNER_SCRATCH = 40


def kernel(owners_ref, slots_ref, g_ref, left_ref, right_ref, out_ref, gm, a, table, inv, spot, table_sem, *scratch):
    x, z, c, y = place()
    others = [device(x, z, 1 - c, y)]
    others += [
        device((x + dx) % NX, z, c, (y + d) % NY) for dx in range(NX) for d in range(NY) if dx or d
    ]
    others += [device(x, (z + d) % NZ, c, y) for d in range(1, NZ)]
    barrier = pltpu.get_barrier_semaphore()
    for other in others:
        pl.semaphore_signal(barrier, inc=1, device_id=other, device_id_type=MESH)

    lane = lax.broadcasted_iota(jnp.int32, (8, 128), 1)

    def note(k, found):
        chip = owners_ref[k] // 2
        spot[k] = (chip % NZ) * 16 + (chip // NZ) * 4 + (owners_ref[k] % 2) * 2 + slots_ref[k]
        return jnp.where(lane == owners_ref[k] * CAP + slots_ref[k], k, found)

    table[...] = lax.fori_loop(0, 64, note, jnp.zeros((8, 128), jnp.int32))
    lookup = pltpu.make_async_copy(table, inv, table_sem)
    lookup.start()
    lookup.wait()
    pl.semaphore_wait(barrier, len(others))
    ring = len(scratch) - OWNER_SCRATCH
    settle = reduce_part(g_ref, left_ref, right_ref, gm, a, *scratch[:ring])
    owner_part(settle, inv, spot, gm, a, out_ref, *scratch[ring:])


def step(owners, slots, grads, left_stats, right_stats):
    vm = pltpu.VMEM
    dma = pltpu.SemaphoreType.DMA
    hbm = pl.BlockSpec(memory_space=pltpu.HBM)
    smem = pl.BlockSpec(memory_space=pltpu.SMEM)
    full, half = vm((512, 512), F32), vm((512, 512), BF16)

    def boxes(count, r):
        return [vm((2, count, 16 * r + 16, 128), I16)] * 2

    ring = [
        vm((1024, 128), F32), vm((16, 128), F32), vm((2, 16, 128), F32),
        vm((8, 32, 32, 128), BF16), vm((8, 32, 32, 128), BF16),
        vm((4, 32, 64, 128), BF16), vm((4, 32, 64, 128), BF16),
        vm((32, 32, 128), F32), vm((32, 64, 128), F32),
        *boxes(7, 32), *boxes(3, 8), *boxes(3, 64), *boxes(7, 8),
        dma((2, 7)), dma((2, 7)), dma((2, 3)), dma((2, 3)),
        dma((2, 3)), dma((2, 3)), dma((2, 7)), dma((2, 7)),
        dma((8,)), dma((4,)), dma((8,)), dma((8,)), dma((4,)), dma((4,)), dma, dma, dma,
    ]
    f_parts, b_parts = len(FORWARD), len(BACK)
    part = vm((b_parts, 16, 64 // b_parts, 128), BF16)
    piece = vm((f_parts, 16, 8 // f_parts, 8, 128), F32)
    owner = [
        piece, piece,
        vm((7, 144, 128), I16), vm((2, 8, 144, 128), I16), vm((2, 8, 16, 8, 128), F32),
        full, half, half, half, half, full,
        half, half, half, half, half, half, half, half,
        vm((2, 2, 512, 512), BF16), half, half,
        part, part, vm((8, 128, 128), BF16), vm((8, 128, 128), BF16), vm((128, 8, 128), F32), vm((1, 1), F32),
        dma((f_parts,)), dma((f_parts,)), dma((7,)), dma((7,)), dma((8,)), dma((8,)),
        dma((2,)), dma((2,)), dma((b_parts,)), dma((b_parts,)), dma((7,)), dma((7,)),
    ]
    assert len(owner) == OWNER_SCRATCH
    return pl.pallas_call(
        kernel,
        out_shape=jax.ShapeDtypeStruct((64, 8, 128), BF16),
        in_specs=[smem, smem, hbm, hbm, hbm],
        out_specs=pl.BlockSpec(memory_space=pltpu.VMEM),
        scratch_shapes=[
            vm((64, 8, 128), F32), full, vm((8, 128), jnp.int32), pltpu.SMEM((8, 128), jnp.int32),
            pltpu.SMEM((64,), jnp.int32), dma, *ring, *owner
        ],
        compiler_params=pltpu.CompilerParams(
            collective_id=0, has_side_effects=True, vmem_limit_bytes=56 * 1024 * 1024
        ),
        name="shampoo_step",
    )(owners, slots, grads, left_stats, right_stats)


def shards(grads, left_stats, right_stats, owners, slots):
    return step(owners, slots, grads, left_stats, right_stats)


def solution(mesh):
    in_specs = (
        P("dp", None, None, "mp"),
        P("dp", None, None, None),
        P("dp", None, None, None),
        P(),
        P(),
    )
    out_specs = P(None, "dp", "mp")
    return jax.shard_map(shards, mesh=mesh, in_specs=in_specs, out_specs=out_specs, check_vma=False)
```
